256 devices in a mesh: rows: 32 (over x, y, core), blk: 8 (over z).
Axes of the slice: x: 4, y: 4, z: 8, core: 2. Of those that a mesh axis runs over, the one named last changes fastest.
Arguments:
- amplitudes: float32 [256, 160000], P('rows', 'blk'), may hold values from -6 to 6
- pair_irrep: int32 [256], P('rows'), may hold values from 0 to 7
- virt_irrep: int32 [400], replicated, may hold values from 0 to 7, as said below
- resid_in: float32 [256, 4864], P('blk', 'rows'), may hold values from -4 to 4
- ladder_ints: float32 [4864, 160000], P('rows', 'blk'), may hold values from -0.0390625 to 0.0390625
Outputs:
- residual: float32 [256, 4864], P('blk', 'rows')
The draws below stay inside these ranges and needn't reach their ends.
Inputs may be any that keep to these rules, and one draw needn't show every extreme that they name: `virt_irrep`: each of the 8 irreps labels exactly 50 virtual orbitals.
All inputs are finite; a program needn't handle non-finite values.
Results may differ from the reference program's by a relative error of at most 0.0001.
Values sent between devices are 32-bit elements; how exact they have to be, the bound alone decides.
No kernel may reach another device: no remote copies, remote signals or barrier semaphores. Data moves between devices by JAX's collectives and lax.ppermute only.
A program may use at most 128 MiB of HBM per device.

```python
import jax
import jax.numpy as jnp
from jax import lax

NV = 400
OP = 256
AB = 4864
CD = 160000


def draw_virt_irrep(key, part):
    key = jax.random.fold_in(key, 11)
    shuffled = jax.random.permutation(key, NV)
    return (shuffled % 8).astype(jnp.int32)


def with_ends(values, stream_key, smallest, largest):
    extent = values.shape
    spot = [jax.random.randint(jax.random.fold_in(stream_key, axis), (), 0, extent[axis]) for axis in range(len(extent))]
    values = values.at[tuple(spot)].set(smallest)
    longest = extent.index(max(extent))
    spot[longest] = (spot[longest] + 1) % extent[longest]
    return values.at[tuple(spot)].set(largest)


def level_of(rng, dims, shards, smallest, largest):
    level = 1.0
    for position, shards_of in shards:
        draws = jax.random.uniform(jax.random.fold_in(jax.random.fold_in(rng, 6), position), (shards_of,), jnp.float32, smallest / len(shards), largest / len(shards))
        level = level * jnp.repeat(jnp.exp(draws), dims[position] // shards_of).reshape((-1,) + (1,) * (len(dims) - 1 - position))
    return level


def gaussian(stream_key, extent, width, bound, shards=(), dtype=jnp.bfloat16):
    array = jax.random.normal(stream_key, extent, jnp.float32) * width
    if len(shards) > 0:
        array = level_of(stream_key, extent, shards, -0.22, 0.18) * array
    return jnp.clip(array, min=-bound, max=bound).astype(dtype)


def setup_inputs(seed: int = 0) -> dict:
    splits = jax.random.split(jax.random.key(seed), 6)
    return {
        "amplitudes": gaussian(splits[0], (OP, CD), 1.0, 6.0, ((0, 32), (1, 8)), jnp.float32),
        "pair_irrep": with_ends(jax.random.randint(splits[1], (OP,), 0, 8), jax.random.fold_in(splits[1], 1), 0, 7).astype(jnp.int32),
        "virt_irrep": draw_virt_irrep(jax.random.fold_in(splits[5], 71), 0),
        "resid_in": gaussian(splits[3], (OP, AB), 0.3, 4.0, ((0, 8), (1, 32)), jnp.float32),
        "ladder_ints": gaussian(splits[4], (AB, CD), (CD // 8) ** -0.5, 0.0390625, ((0, 32), (1, 8)), jnp.float32),
    }


def reference(amplitudes, pair_irrep, virt_irrep, resid_in, ladder_ints):
    def add_block(c_index, total):
        amp_block = lax.dynamic_slice_in_dim(amplitudes, c_index * NV, NV, 1)
        int_block = lax.dynamic_slice_in_dim(ladder_ints, c_index * NV, NV, 1)
        c_irrep = lax.dynamic_slice_in_dim(virt_irrep, c_index, 1, 0)
        sector = jnp.bitwise_xor(c_irrep, virt_irrep)
        allowed = jnp.where(sector[None, :] == pair_irrep[:, None], amp_block, jnp.zeros_like(amp_block))
        return total + lax.dot_general(allowed, int_block, (((1,), (1,)), ((), ())), precision=lax.Precision.HIGHEST, preferred_element_type=jnp.float32)

    ladder = lax.fori_loop(0, NV, add_block, jnp.zeros((OP, AB), jnp.float32))
    return resid_in + ladder
```

```python
import functools

import jax
import jax.numpy as jnp
from jax import lax
from jax.experimental import pallas as pl
from jax.experimental.pallas import tpu as pltpu
from jax.sharding import PartitionSpec as P

BF = jnp.bfloat16
F32 = jnp.float32
I32 = jnp.int32

NV = 400
NI = 8
PER = 50
CN = 50
WIN = 512
OJ = 8
OP = 256
ABD = 152
ABP = 160
PAY = 2560
GRP = 10
LW = 2048
CD = CN * NV
HOPS = (0, 2, 1, 3)
VMEM_LIMIT = 56 * 1024 * 1024


def nt(a, b):
    return lax.dot_general(a, b, (((1,), (1,)), ((), ())), preferred_element_type=F32)


def split(x):
    hi = x.astype(BF)
    return hi, (x - hi.astype(F32)).astype(BF)


def where_in_lanes(lane, pieces):
    out = pieces[-1][1]
    for edge, x in reversed(pieces[:-1]):
        out = jnp.where(lane < edge, x, out)
    return out


def compact_kernel(blk, virt_s, pair_s, virt_v, amp, pay, aux):
    c0 = blk() * CN
    lane = lax.broadcasted_iota(I32, (8, WIN), 1)
    sub = lax.broadcasted_iota(I32, (8, WIN), 0)
    irrep = jnp.concatenate([virt_v[...], jnp.full((1, WIN - NV), -1, I32)], axis=1)
    irrep = jnp.broadcast_to(irrep, (8, WIN))
    member = irrep == sub
    before = lax.broadcasted_iota(I32, (WIN, WIN), 0) < lax.broadcasted_iota(I32, (WIN, WIN), 1)
    count = jnp.dot(
        jnp.where(member, 1.0, 0.0).astype(BF),
        jnp.where(before, 1.0, 0.0).astype(BF),
        preferred_element_type=F32,
    )
    rank = jnp.sum(jnp.where(member, count, 0.0), axis=0, keepdims=True).astype(I32)
    rank = jnp.where(lane < NV, jnp.broadcast_to(rank, (8, WIN)), -1)
    aux[0:8, :] = rank
    aux[8:16, :] = irrep
    pair = jnp.zeros((8, WIN), I32)
    for i in range(OJ):
        pair = jnp.where(sub == i, pair_s[i], pair)
    need = jnp.where(lane < NV, jnp.bitwise_xor(irrep, pair), -1)
    row = lax.broadcasted_iota(I32, (128, WIN), 0)
    rows = {}
    for v in range(8):
        need_v = pltpu.roll(need, 16 * v, 1) if v else need
        rank_v = pltpu.roll(rank, 16 * v, 1) if v else rank
        pick = jnp.where(jnp.broadcast_to(rank_v[0:1, :], (128, WIN)) == row, 1.0, 0.0).astype(BF)
        cs = list(range(v, CN, 8))
        xs = []
        for c in cs:
            first = (NV * c) // 128 * 128
            width = min(WIN, CD - first)
            x = amp[:, first : first + width]
            if width < WIN:
                x = jnp.concatenate([x, jnp.zeros((8, WIN - width), F32)], axis=1)
            xs.append(jnp.where(need_v == virt_s[c0 + c], x, 0.0))
        if len(xs) % 2:
            xs.append(jnp.zeros((8, WIN), F32))
        hi, lo = split(jnp.concatenate(xs, axis=0))
        r = nt(hi, pick) + nt(lo, pick)
        for i, c in enumerate(cs):
            rows[c] = r[8 * i : 8 * i + 8, :]
    lane = lax.broadcasted_iota(I32, (8, 128), 1)
    for q in range(GRP):
        r0, r1, r2, r3, r4 = (rows[5 * q + e] for e in range(5))
        r1 = pltpu.roll(r1, 50, 1)
        r2a = pltpu.roll(r2, 100, 1)
        r2b = pltpu.roll(r2, 103, 1)
        r3 = pltpu.roll(r3, 25, 1)
        r4 = pltpu.roll(r4, 75, 1)
        a = where_in_lanes(lane, [(50, r0), (100, r1), (125, r2a), (128, jnp.zeros_like(r0))])
        b = where_in_lanes(lane, [(25, r2b), (75, r3), (128, r4)])
        if q == GRP - 1:
            b = jnp.where(lane == 127, pair[:, 0:128].astype(F32), b)
        pay[:, 256 * q : 256 * q + 128] = a
        pay[:, 256 * q + 128 : 256 * q + 256] = b


def sort_kernel(blk, q0, nq, virt_s, aux, tail, main, lhi, llo, b, m):
    g = pl.program_id(0)
    q = g + q0
    c0 = blk() * CN

    b[ABD - 8 : ABP, :] = jnp.zeros((ABP - ABD + 8, 2560), BF)
    b[ABP + ABD - 8 : 2 * ABP, :] = jnp.zeros((ABP - ABD + 8, 2560), BF)
    for first, width, src in ((0, 512, tail), (512, LW, main)):
        x = src[...]
        if q0 + nq == GRP and src is main:
            at = lax.broadcasted_iota(I32, (ABD, width), 1) + LW * q
            x = jnp.where(at < CD, x, 0.0)
        hi, lo = split(x)
        b[0:ABD, first : first + width] = hi
        b[ABP : ABP + ABD, first : first + width] = lo
    row = lax.broadcasted_iota(I32, (128, WIN), 0)
    parts = []
    for e in range(5):
        start = 512 + NV * e - 48 * q
        first = pl.multiple_of(start // 128 * 128, 128)
        shift = start - first
        rank = pltpu.roll(aux[0:8, :], shift, 1)
        irrep = pltpu.roll(aux[8:16, :], shift, 1)
        inside = rank >= 0
        sector = jnp.bitwise_xor(irrep, virt_s[c0 + 5 * q + e])
        place = rank + 50 * e
        place = jnp.where(place >= 125, place - 125, place)
        place = jnp.bitwise_and(place + 64 * jnp.bitwise_and(sector, 1), 127)
        place = jnp.where(inside, place, -1)
        pick = jnp.where(jnp.broadcast_to(place[0:1, :], (128, WIN)) == row, 1.0, 0.0).astype(BF)
        half = jnp.where(inside, lax.shift_right_logical(sector, 1), -1)
        for u in range(4):
            on = jnp.where(half[0:1, :] == u, 1.0, 0.0).astype(BF)
            m[128 * u : 128 * u + 128, :] = pick * jnp.broadcast_to(on, (128, WIN))
        parts.append(nt(b[:, pl.ds(first, WIN)], m[...]))
    lane = lax.broadcasted_iota(I32, (2 * ABP, 128), 1)
    turned = jnp.bitwise_and(lane + 64, 127)
    for u in range(4):
        r = [p[:, 128 * u : 128 * u + 128] for p in parts]
        for odd in range(2):
            at = turned if odd else lane
            for t in range(2):
                edges = [(50, r[0]), (100, r[1]), (128, r[2])] if t == 0 else [(25, r[2]), (75, r[3]), (128, r[4])]
                x = where_in_lanes(at, edges)
                if odd:
                    x = pltpu.roll(x, 64, 1)
                x = x.astype(BF)
                lhi[2 * u + odd, :, 128 * t : 128 * t + 128] = x[0:ABP]
                llo[2 * u + odd, :, 128 * t : 128 * t + 128] = x[ABP : 2 * ABP]


def main_kernel(rows, widths, *refs):
    n = len(widths)
    pieces = refs[:8]
    ls = refs[8 : 8 + 2 * n]
    out, gath, ghi, glo, acc, pair, sems = refs[8 + 2 * n :]
    s = pl.program_id(0)

    @pl.when(s == 0)
    def _():
        me = rows()
        core, y, x = me % 2, (me // 2) % 4, me // 8
        copies = []
        for j in range(8):
            far = j // 4
            kind = jnp.where(far == 1, 1 - core, core)
            d2 = HOPS[j % 4]
            for i in range(4):
                d1 = HOPS[i]
                dx = jnp.where(kind == 0, d1, d2)
                dy = jnp.where(kind == 0, d2, d1)
                xx = (x + 4 - dx) % 4
                yy = (y + 4 - dy) % 4
                shard = (xx * 4 + yy) * 2 + kind
                at = pl.multiple_of(shard * OJ, OJ)
                copies.append(
                    pltpu.make_async_copy(pieces[j].at[pl.ds(8 * i, 8), :], gath.at[pl.ds(at, OJ), :], sems.at[j, i])
                )
        for c in copies:
            c.start()
        for c in copies:
            c.wait()
        for k in range(0, PAY, 512):
            hi, lo = split(gath[:, k : k + 512])
            ghi[:, k : k + 512] = hi
            glo[:, k : k + 512] = lo
        last = gath[:, PAY - 128 : PAY]
        pair[...] = jnp.transpose(last)[120:128, :]
        acc[...] = jnp.zeros_like(acc)

    total = jnp.zeros((ABP, OP), F32)
    k = 0
    for i, w in enumerate(widths):
        hi = ls[2 * i][0]
        lo = ls[2 * i + 1][0]
        total = total + nt(hi, ghi[:, k : k + w])
        total = total + nt(lo, ghi[:, k : k + w])
        total = total + nt(hi, glo[:, k : k + w])
        k += w
    mine = jnp.broadcast_to(pair[7:8, :], (ABP, OP)) == s.astype(F32)
    acc[...] += jnp.where(mine, total, 0.0)

    @pl.when(s == NI - 1)
    def _():
        out[...] = jnp.transpose(acc[...])[:, 0:ABD]


def smem():
    return pl.BlockSpec(memory_space=pltpu.SMEM)


def compact(blk, virt, pair, amp):
    vmem = pl.BlockSpec(memory_space=pltpu.VMEM)
    return pl.pallas_call(
        functools.partial(compact_kernel, blk),
        out_shape=(jax.ShapeDtypeStruct((OJ, PAY), F32), jax.ShapeDtypeStruct((16, WIN), I32)),
        in_specs=[smem(), smem(), vmem, vmem],
        out_specs=(vmem, vmem),
        compiler_params=pltpu.CompilerParams(vmem_limit_bytes=VMEM_LIMIT),
        name="compact",
    )(virt, pair, virt.reshape(1, NV), amp)


def sort_part(blk, q0, nq, virt, aux, ints):
    shape = jax.ShapeDtypeStruct((NI, ABP, 256 * nq), BF)
    return pl.pallas_call(
        functools.partial(sort_kernel, blk, q0, nq),
        out_shape=(shape, shape),
        grid=(nq,),
        in_specs=[
            smem(),
            pl.BlockSpec((16, WIN), lambda g: (0, 0)),
            pl.BlockSpec((ABD, 512), lambda g: (0, jnp.maximum(4 * (g + q0) - 1, 0))),
            pl.BlockSpec((ABD, LW), lambda g: (0, g + q0)),
        ],
        out_specs=(
            pl.BlockSpec((NI, ABP, 256), lambda g: (0, 0, g)),
            pl.BlockSpec((NI, ABP, 256), lambda g: (0, 0, g)),
        ),
        scratch_shapes=[pltpu.VMEM((2 * ABP, 2560), BF), pltpu.VMEM((512, WIN), BF)],
        compiler_params=pltpu.CompilerParams(vmem_limit_bytes=VMEM_LIMIT),
        cost_estimate=pl.CostEstimate(flops=nq * 5 * 2 * 320 * 512 * 512, bytes_accessed=nq * 3000000, transcendentals=0),
        name="sort_ints",
    )(virt, aux, ints, ints)


def contract(rows, pieces, parts):
    widths = tuple(p[0].shape[2] for p in parts)
    flat = [x for p in parts for x in p]
    return pl.pallas_call(
        functools.partial(main_kernel, rows, widths),
        out_shape=jax.ShapeDtypeStruct((OP, ABD), F32),
        grid=(NI,),
        in_specs=[pl.BlockSpec(memory_space=pl.ANY)] * 8
        + [pl.BlockSpec((1, ABP, x.shape[2]), lambda s: (s, 0, 0)) for x in flat],
        out_specs=pl.BlockSpec((OP, ABD), lambda s: (0, 0)),
        scratch_shapes=[
            pltpu.VMEM((OP, PAY), F32),
            pltpu.VMEM((OP, PAY), BF),
            pltpu.VMEM((OP, PAY), BF),
            pltpu.VMEM((ABP, OP), F32),
            pltpu.VMEM((8, OP), F32),
            pltpu.SemaphoreType.DMA((8, 4)),
        ],
        compiler_params=pltpu.CompilerParams(vmem_limit_bytes=VMEM_LIMIT),
        cost_estimate=pl.CostEstimate(flops=3 * 2 * 1280 * 2560 * 256, bytes_accessed=16000000, transcendentals=0),
        name="contract",
    )(*pieces, *flat)


def at(x, y, core):
    return ((x % 4) * 4 + y % 4) * 2 + core


def walk(hop, second):
    pairs = []
    for x in range(4):
        for y in range(4):
            for core in range(2):
                along_x = (core == 0) != second
                to = at(x + hop, y, core) if along_x else at(x, y + hop, core)
                pairs.append((at(x, y, core), to))
    return pairs


SWAP = [(i, i ^ 1) for i in range(32)]


def body(amplitudes, pair_irrep, virt_irrep, resid_in, ladder_ints):
    blk = functools.partial(lax.axis_index, "blk")
    rows = functools.partial(lax.axis_index, "rows")
    pay, aux = compact(blk, virt_irrep, pair_irrep, amplitudes)
    first = [pay] + [lax.ppermute(pay, "rows", walk(h, False)) for h in HOPS[1:]]
    parts = [sort_part(blk, 0, 3, virt_irrep, aux, ladder_ints)]
    four = jnp.concatenate(first, axis=0)
    near = [four] + [lax.ppermute(four, "rows", walk(h, True)) for h in HOPS[1:]]
    parts.append(sort_part(blk, 3, 4, virt_irrep, aux, ladder_ints))
    far = [lax.ppermute(p, "rows", SWAP) for p in near]
    parts.append(sort_part(blk, 7, 3, virt_irrep, aux, ladder_ints))
    terms = contract(rows, near + far, parts)
    got = lax.all_to_all(terms.reshape(8, 32, ABD), "blk", 0, 0)
    return resid_in + jnp.sum(got, axis=0)


def solution(mesh):
    placed = (P("rows", "blk"), P("rows"), P(), P("blk", "rows"), P("rows", "blk"))
    return jax.shard_map(
        body, mesh=mesh, in_specs=placed, out_specs=P("blk", "rows"), check_vma=False
    )
```

```python
import functools

import jax
import jax.numpy as jnp
from jax import lax
from jax.experimental import pallas as pl
from jax.experimental.pallas import tpu as pltpu
from jax.sharding import PartitionSpec as P

BF = jnp.bfloat16
F32 = jnp.float32
I32 = jnp.int32

NV = 400
NI = 8
PER = 50
CN = 50
WIN = 512
OJ = 8
OP = 256
ABD = 152
ABP = 160
PAY = 2560
GRP = 10
GW = 2048
SPAN = 2176
CD = CN * NV
EDGE = CD // 128 * 128
CHIPS = 16
SECT = 4
VMEM_LIMIT = 24 * 1024 * 1024
SORT_VMEM = 34 * 1024 * 1024


def nt(a, b):
    return lax.dot_general(a, b, (((1,), (1,)), ((), ())), preferred_element_type=F32)


def split(x):
    hi = x.astype(BF)
    return hi, (x - hi.astype(F32)).astype(BF)


def where_in_lanes(lane, pieces):
    out = pieces[-1][1]
    for edge, x in reversed(pieces[:-1]):
        out = jnp.where(lane < edge, x, out)
    return out


def turn(lane, x):
    moved = jnp.where(lane < 62, pltpu.roll(x, 65, 1), pltpu.roll(x, 62, 1))
    return jnp.where(lane < 125, moved, 0.0)


def compact_kernel(blk, virt_s, pair_s, virt_v, amp, edge, pays, aux, tail, pay, sem):
    c0 = blk() * CN
    lane = lax.broadcasted_iota(I32, (8, WIN), 1)
    sub = lax.broadcasted_iota(I32, (8, WIN), 0)
    irrep = jnp.concatenate([virt_v[...], jnp.full((1, WIN - NV), -1, I32)], axis=1)
    irrep = jnp.broadcast_to(irrep, (8, WIN))
    member = irrep == sub
    before = lax.broadcasted_iota(I32, (WIN, WIN), 0) < lax.broadcasted_iota(I32, (WIN, WIN), 1)
    count = jnp.dot(
        jnp.where(member, 1.0, 0.0).astype(BF),
        jnp.where(before, 1.0, 0.0).astype(BF),
        preferred_element_type=F32,
    )
    rank = jnp.sum(jnp.where(member, count, 0.0), axis=0, keepdims=True).astype(I32)
    rank = jnp.where(lane < NV, jnp.broadcast_to(rank, (8, WIN)), -1)
    aux[0:8, :] = rank
    aux[8:16, :] = irrep
    tail[...] = jnp.where(lax.broadcasted_iota(I32, (ABD, 128), 1) < CD - EDGE, edge[...], 0.0)
    pair = jnp.zeros((8, WIN), I32)
    for i in range(OJ):
        pair = jnp.where(sub == i, pair_s[i], pair)
    need = jnp.where(lane < NV, jnp.bitwise_xor(irrep, pair), -1)
    row = lax.broadcasted_iota(I32, (128, WIN), 0)
    rows = {}
    for v in range(8):
        need_v = pltpu.roll(need, 16 * v, 1) if v else need
        rank_v = pltpu.roll(rank, 16 * v, 1) if v else rank
        pick = jnp.where(jnp.broadcast_to(rank_v[0:1, :], (128, WIN)) == row, 1.0, 0.0).astype(BF)
        cs = list(range(v, CN, 8))
        xs = []
        for c in cs:
            first = (NV * c) // 128 * 128
            width = min(WIN, CD - first)
            x = amp[:, first : first + width]
            if width < WIN:
                x = jnp.concatenate([x, jnp.zeros((8, WIN - width), F32)], axis=1)
            xs.append(jnp.where(need_v == virt_s[c0 + c], x, 0.0))
        if len(xs) % 2:
            xs.append(jnp.zeros((8, WIN), F32))
        hi, lo = split(jnp.concatenate(xs, axis=0))
        r = nt(hi, pick) + nt(lo, pick)
        for i, c in enumerate(cs):
            rows[c] = r[8 * i : 8 * i + 8, :]
    lane = lax.broadcasted_iota(I32, (8, 128), 1)
    odd = jnp.bitwise_and(pair[:, 0:128], 1) == 1
    for q in range(GRP):
        r0, r1, r2, r3, r4 = (rows[5 * q + e] for e in range(5))
        r1 = pltpu.roll(r1, 50, 1)
        r2a = pltpu.roll(r2, 100, 1)
        r2b = pltpu.roll(r2, 103, 1)
        r3 = pltpu.roll(r3, 25, 1)
        r4 = pltpu.roll(r4, 75, 1)
        a = where_in_lanes(lane, [(50, r0), (100, r1), (125, r2a), (128, jnp.zeros_like(r0))])
        b = where_in_lanes(lane, [(25, r2b), (75, r3), (128, r4)])
        a = jnp.where(odd, turn(lane, a), a)
        b = jnp.where(odd, turn(lane, b), b)
        if q == GRP - 1:
            b = jnp.where(lane == 127, pair[:, 0:128].astype(F32), b)
        pay[:, 256 * q : 256 * q + 128] = a
        pay[:, 256 * q + 128 : 256 * q + 256] = b
    copies = [pltpu.make_async_copy(pay, pays.at[j], sem.at[j]) for j in range(CHIPS)]
    for c in copies:
        c.start()
    for c in copies:
        c.wait()


def chunk(q0, nq, i):
    q = q0 + i
    first = GW * q + (128 if i else 0) if i else NV * 5 * q0 // 128 * 128
    last = min(GW * (q + 1) + 128, EDGE)
    return first, last - first


def sort_kernel(blk, q0, nq, virt_s, aux, tail, ints, lhi, llo, x, ba, bb, ma, mb, sems):
    c0 = blk() * CN
    base = chunk(q0, nq, 0)[0]
    copies = []
    for i in range(nq):
        first, width = chunk(q0, nq, i)
        copies.append(
            pltpu.make_async_copy(
                ints.at[:, pl.ds(first, width)], x.at[:, pl.ds(first - base, width)], sems.at[i]
            )
        )
    for c in copies[:4]:
        c.start()
    if q0 + nq == GRP:
        x[:, EDGE - base : EDGE - base + 128] = tail[...]
    for b in (ba, bb):
        b[ABD - 8 : ABP, :] = jnp.zeros((ABP - ABD + 8, SPAN), BF)
        b[ABP + ABD - 8 : 2 * ABP, :] = jnp.zeros((ABP - ABD + 8, SPAN), BF)
    row = lax.broadcasted_iota(I32, (128, WIN), 0)
    lane = lax.broadcasted_iota(I32, (2 * ABP, 128), 1)
    turned = jnp.where(lane < 62, lane + 63, lane - 62).astype(F32).astype(BF)
    lane = lane.astype(F32).astype(BF)

    def load(i, b):
        begin = pl.multiple_of(NV * 5 * (q0 + i) // 128 * 128 - base, 128)
        hi, lo = split(x[:, pl.ds(begin, SPAN)])
        b[0:ABD, :] = hi
        b[ABP : ABP + ABD, :] = lo

    def sort(i, e, b, m):
        start = NV * 5 * (q0 + i)
        at = start - start // 128 * 128 + NV * e
        first = pl.multiple_of(at // 128 * 128, 128)
        rank = pltpu.roll(aux[0:8, :], at - first, 1)
        irrep = pltpu.roll(aux[8:16, :], at - first, 1)
        inside = rank >= 0
        sector = jnp.bitwise_xor(irrep, virt_s[c0 + 5 * (q0 + i) + e])
        place = rank + 50 * e
        place = jnp.where(place >= 125, place - 125, place)
        place = place + 62 * jnp.bitwise_and(sector, 1)
        place = jnp.where(place >= 125, place - 125, place)
        place = jnp.where(inside, place, -1)
        pick = jnp.where(jnp.broadcast_to(place[0:1, :], (128, WIN)) == row, 1.0, 0.0).astype(BF)
        half = jnp.where(inside, lax.shift_right_logical(sector, 1), -1)
        for u in range(4):
            on = jnp.where(half[0:1, :] == u, 1.0, 0.0).astype(BF)
            m[e, 128 * u : 128 * u + 128, :] = pick * jnp.broadcast_to(on, (128, WIN))
        return nt(b[:, pl.ds(first, WIN)], m[e]).astype(BF)

    def merge(i, u, parts):
        to = pl.multiple_of(256 * i, 256)
        r = [p[:, 128 * u : 128 * u + 128] for p in parts]
        for odd in range(2):
            at = turned if odd else lane
            for t in range(2):
                edges = [(50, r[0]), (100, r[1]), (128, r[2])] if t == 0 else [(25, r[2]), (75, r[3]), (128, r[4])]
                y = where_in_lanes(at, edges)
                lhi[2 * u + odd, :, pl.ds(to + 128 * t, 128)] = y[0:ABP]
                llo[2 * u + odd, :, pl.ds(to + 128 * t, 128)] = y[ABP : 2 * ABP]

    def pair(k, carry):
        i = 2 * k
        for j, c in enumerate(copies):
            pl.when(k == j // 2)(c.wait)
            if j >= 4:
                pl.when(k == j // 2 - 2)(c.start)
        load(i, ba)
        load(i + 1, bb)
        pa = [sort(i, e, ba, ma) for e in range(5)]
        pb = []
        for e in range(5):
            pb.append(sort(i + 1, e, bb, mb))
            if e < 4:
                merge(i, e, pa)
        for u in range(4):
            merge(i + 1, u, pb)
        return carry

    lax.fori_loop(0, nq // 2, pair, 0)


def main_kernel(core, widths, near, far, *refs):
    n = len(widths)
    ls = refs[: 2 * n]
    out, gath, ghi, glo, acc, pair, sems = refs[2 * n :]
    mine = core()
    copies = [
        pltpu.make_async_copy(src, gath.at[pl.ds(pl.multiple_of(half * 128, 128), 128), :], sems.at[i])
        for i, (src, half) in enumerate(((near, mine), (far, 1 - mine)))
    ]
    for c in copies:
        c.start()
    for c in copies:
        c.wait()
    for k in range(0, PAY, 512):
        hi, lo = split(gath[:, k : k + 512])
        ghi[:, k : k + 512] = hi
        glo[:, k : k + 512] = lo
    pair[...] = jnp.transpose(gath[:, PAY - 128 : PAY])[120:128, :]
    acc[...] = jnp.zeros_like(acc)

    def quarter(step, carry):
        total = None
        k = 0
        for i, w in enumerate(widths):
            hi = ls[2 * i][pl.ds(SECT * step, SECT)].reshape(SECT * ABP, w)
            lo = ls[2 * i + 1][pl.ds(SECT * step, SECT)].reshape(SECT * ABP, w)
            x = nt(hi, ghi[:, k : k + w]) + nt(lo, ghi[:, k : k + w]) + nt(hi, glo[:, k : k + w])
            total = x if total is None else total + x
            k += w
        part = acc[...]
        for i in range(SECT):
            own = jnp.broadcast_to(pair[7:8, :], (ABP, OP)) == (SECT * step + i).astype(F32)
            part = part + jnp.where(own, total[ABP * i : ABP * i + ABP, :], 0.0)
        acc[...] = part
        return carry

    lax.fori_loop(0, NI // SECT, quarter, 0)
    t = jnp.transpose(acc[...])
    for j in range(16):
        for c in range(2):
            out[16 * j + 8 * c : 16 * j + 8 * c + 8, :] = t[128 * c + 8 * j : 128 * c + 8 * j + 8, 0:ABD]


def smem():
    return pl.BlockSpec(memory_space=pltpu.SMEM)


def whole(shape):
    return pl.BlockSpec(shape, lambda g: (0,) * len(shape))


def compact(blk, virt, pair, amp, ints):
    return pl.pallas_call(
        functools.partial(compact_kernel, blk),
        out_shape=(
            jax.ShapeDtypeStruct((CHIPS, OJ, PAY), F32),
            jax.ShapeDtypeStruct((16, WIN), I32),
            jax.ShapeDtypeStruct((ABD, 128), F32),
        ),
        grid=(1,),
        in_specs=[
            smem(),
            smem(),
            whole((1, NV)),
            whole((OJ, CD)),
            pl.BlockSpec((ABD, 128), lambda g: (0, EDGE // 128)),
        ],
        out_specs=(pl.BlockSpec(memory_space=pl.ANY), whole((16, WIN)), whole((ABD, 128))),
        scratch_shapes=[pltpu.VMEM((OJ, PAY), F32), pltpu.SemaphoreType.DMA((CHIPS,))],
        compiler_params=pltpu.CompilerParams(vmem_limit_bytes=VMEM_LIMIT),
        name="compact",
    )(virt, pair, virt.reshape(1, NV), amp, ints)


def sort_part(blk, q0, nq, virt, aux, tail, ints):
    shape = pltpu.VMEM((NI, ABP, 256 * nq), BF)
    vmem = pl.BlockSpec(memory_space=pltpu.VMEM)
    begin = chunk(q0, nq, 0)[0]
    end = NV * 5 * (q0 + nq - 1) // 128 * 128 + SPAN
    end = max(end, sum(chunk(q0, nq, nq - 1)))
    return pl.pallas_call(
        functools.partial(sort_kernel, blk, q0, nq),
        out_shape=(shape, shape),
        in_specs=[smem(), vmem, vmem, pl.BlockSpec(memory_space=pl.ANY)],
        out_specs=(vmem, vmem),
        scratch_shapes=[
            pltpu.VMEM((ABD, end - begin), F32),
            pltpu.VMEM((2 * ABP, SPAN), BF),
            pltpu.VMEM((2 * ABP, SPAN), BF),
            pltpu.VMEM((5, 512, WIN), BF),
            pltpu.VMEM((5, 512, WIN), BF),
            pltpu.SemaphoreType.DMA((nq,)),
        ],
        compiler_params=pltpu.CompilerParams(vmem_limit_bytes=SORT_VMEM),
        cost_estimate=pl.CostEstimate(flops=nq * 5 * 2 * 320 * 512 * 512, bytes_accessed=nq * 1300000, transcendentals=0),
        name="sort_ints",
    )(virt, aux, tail, ints)


def contract(core, near, far, parts):
    widths = tuple(p[0].shape[2] for p in parts)
    flat = [x for p in parts for x in p]
    vmem = pl.BlockSpec(memory_space=pltpu.VMEM)
    return pl.pallas_call(
        functools.partial(main_kernel, core, widths),
        out_shape=jax.ShapeDtypeStruct((OP, ABD), F32),
        in_specs=[pl.BlockSpec(memory_space=pl.ANY)] * 2 + [vmem] * len(flat),
        out_specs=vmem,
        scratch_shapes=[
            pltpu.VMEM((OP, PAY), F32),
            pltpu.VMEM((OP, PAY), BF),
            pltpu.VMEM((OP, PAY), BF),
            pltpu.VMEM((ABP, OP), F32),
            pltpu.VMEM((8, OP), F32),
            pltpu.SemaphoreType.DMA((2,)),
        ],
        compiler_params=pltpu.CompilerParams(vmem_limit_bytes=VMEM_LIMIT),
        cost_estimate=pl.CostEstimate(flops=3 * 2 * 1280 * 2560 * 256, bytes_accessed=16000000, transcendentals=0),
        name="contract",
    )(near, far, *[pltpu.with_memory_space_constraint(x, pltpu.VMEM) for x in flat])


SWAP = [(i, i ^ 1) for i in range(32)]
PLANE = [[2 * chip + core for chip in range(CHIPS)] for core in range(2)]


def body(amplitudes, pair_irrep, virt_irrep, resid_in, ladder_ints):
    blk = functools.partial(lax.axis_index, "blk")
    pays, aux, tail = compact(blk, virt_irrep, pair_irrep, amplitudes, ladder_ints)
    near = lax.all_to_all(pays, "rows", 0, 0, axis_index_groups=PLANE).reshape(CHIPS * OJ, PAY)
    parts = [sort_part(blk, 0, 8, virt_irrep, aux, tail, ladder_ints)]
    far = lax.ppermute(near, "rows", SWAP)
    parts.append(sort_part(blk, 8, 2, virt_irrep, aux, tail, ladder_ints))
    terms = contract(lambda: lax.axis_index("rows") % 2, near, far, parts)
    got = lax.all_to_all(terms.reshape(8, 32, ABD), "blk", 0, 0)
    return resid_in + jnp.sum(got, axis=0)


def solution(mesh):
    placed = (P("rows", "blk"), P("rows"), P(), P("blk", "rows"), P("rows", "blk"))
    return jax.shard_map(
        body, mesh=mesh, in_specs=placed, out_specs=P("blk", "rows"), check_vma=False
    )
```

```python
import functools

import jax
import jax.numpy as jnp
from jax import lax
from jax.experimental import pallas as pl
from jax.experimental.pallas import tpu as pltpu
from jax.sharding import PartitionSpec as P

BF = jnp.bfloat16
F32 = jnp.float32
I32 = jnp.int32

NV = 400
NI = 8
PER = 50
CN = 50
WIN = 512
OJ = 8
OP = 256
ABD = 152
ABP = 160
PAY = 2560
GRP = 10
SPAN = 2176
HEAD = 4224
CD = CN * NV
EDGE = CD // 128 * 128
HOPS = (0, 2, 1, 3)
PARTS = ((0, 2), (2, 6), (8, 2))
SECT = 4
VMEM_LIMIT = 24 * 1024 * 1024
COMPACT_VMEM = 56 * 1024 * 1024
SORT_VMEM = 32 * 1024 * 1024


def nt(a, b):
    return lax.dot_general(a, b, (((1,), (1,)), ((), ())), preferred_element_type=F32)


def split(x):
    hi = x.astype(BF)
    return hi, (x - hi.astype(F32)).astype(BF)


def where_in_lanes(lane, pieces):
    out = pieces[-1][1]
    for edge, x in reversed(pieces[:-1]):
        out = jnp.where(lane < edge, x, out)
    return out


def turn(lane, x):
    moved = jnp.where(lane < 62, pltpu.roll(x, 65, 1), pltpu.roll(x, 62, 1))
    return jnp.where(lane < 125, moved, 0.0)


def compact_kernel(blk, virt_s, pair_s, virt_v, amps, ints, edge, pays, four, aux, tail, head, amp, pay, sems):
    load = pltpu.make_async_copy(amps, amp, sems.at[0])
    load.start()
    ahead = pltpu.make_async_copy(ints.at[:, pl.ds(0, HEAD)], head, sems.at[1])
    ahead.start()
    c0 = blk() * CN
    lane = lax.broadcasted_iota(I32, (8, WIN), 1)
    sub = lax.broadcasted_iota(I32, (8, WIN), 0)
    irrep = jnp.concatenate([virt_v[...], jnp.full((1, WIN - NV), -1, I32)], axis=1)
    irrep = jnp.broadcast_to(irrep, (8, WIN))
    member = irrep == sub
    before = lax.broadcasted_iota(I32, (WIN, WIN), 0) < lax.broadcasted_iota(I32, (WIN, WIN), 1)
    count = jnp.dot(
        jnp.where(member, 1.0, 0.0).astype(BF),
        jnp.where(before, 1.0, 0.0).astype(BF),
        preferred_element_type=F32,
    )
    rank = jnp.sum(jnp.where(member, count, 0.0), axis=0, keepdims=True).astype(I32)
    rank = jnp.where(lane < NV, jnp.broadcast_to(rank, (8, WIN)), -1)
    tail[...] = jnp.where(lax.broadcasted_iota(I32, (ABD, 128), 1) < CD - EDGE, edge[...], 0.0)
    pair = jnp.zeros((8, WIN), I32)
    for i in range(OJ):
        pair = jnp.where(sub == i, pair_s[i], pair)
    need = jnp.where(lane < NV, jnp.bitwise_xor(irrep, pair), -1)
    row = lax.broadcasted_iota(I32, (128, WIN), 0)
    rows = {}
    load.wait()
    for v in range(8):
        need_v = pltpu.roll(need, 16 * v, 1) if v else need
        rank_v = pltpu.roll(rank, 16 * v, 1) if v else rank
        aux[v, 0:8, :] = rank_v
        aux[v, 8:16, :] = pltpu.roll(irrep, 16 * v, 1) if v else irrep
        pick = jnp.where(jnp.broadcast_to(rank_v[0:1, :], (128, WIN)) == row, 1.0, 0.0).astype(BF)
        cs = list(range(v, CN, 8))
        xs = []
        for c in cs:
            first = (NV * c) // 128 * 128
            width = min(WIN, CD - first)
            x = amp[:, first : first + width]
            if width < WIN:
                x = jnp.concatenate([x, jnp.zeros((8, WIN - width), F32)], axis=1)
            xs.append(jnp.where(need_v == virt_s[c0 + c], x, 0.0))
        if len(xs) % 2:
            xs.append(jnp.zeros((8, WIN), F32))
        hi, lo = split(jnp.concatenate(xs, axis=0))
        r = nt(hi, pick) + nt(lo, pick)
        for i, c in enumerate(cs):
            rows[c] = r[8 * i : 8 * i + 8, :]
    lane = lax.broadcasted_iota(I32, (8, 128), 1)
    odd = jnp.bitwise_and(pair[:, 0:128], 1) == 1
    for q in range(GRP):
        r0, r1, r2, r3, r4 = (rows[5 * q + e] for e in range(5))
        r1 = pltpu.roll(r1, 50, 1)
        r2a = pltpu.roll(r2, 100, 1)
        r2b = pltpu.roll(r2, 103, 1)
        r3 = pltpu.roll(r3, 25, 1)
        r4 = pltpu.roll(r4, 75, 1)
        a = where_in_lanes(lane, [(50, r0), (100, r1), (125, r2a), (128, jnp.zeros_like(r0))])
        b = where_in_lanes(lane, [(25, r2b), (75, r3), (128, r4)])
        a = jnp.where(odd, turn(lane, a), a)
        b = jnp.where(odd, turn(lane, b), b)
        if q == GRP - 1:
            b = jnp.where(lane == 127, pair[:, 0:128].astype(F32), b)
        pay[:, 256 * q : 256 * q + 128] = a
        pay[:, 256 * q + 128 : 256 * q + 256] = b
    copies = [
        pltpu.make_async_copy(pay, pays, sems.at[2]),
        pltpu.make_async_copy(pay, four.at[pl.ds(0, OJ), :], sems.at[3]),
    ]
    for c in copies:
        c.start()
    for c in copies:
        c.wait()
    ahead.wait()


def start_of(q):
    return NV * 5 * q // 128 * 128


def chunks(q0, nq):
    edges = [start_of(q0 + 2)] + [min(start_of(q) + SPAN, EDGE) for q in range(q0 + 3, q0 + nq, 2)]
    return [(a, b - a) for a, b in zip(edges, edges[1:])]


def sort_kernel(blk, q0, nq, virt_s, aux, tail, head, ints, *refs):
    lhi, llo, done = refs[:3]
    x, ba, bb, ma, mb, sems = refs[-6:]
    c0 = blk() * CN
    spans = chunks(q0, nq)
    base = start_of(q0 + 2)
    copies = [
        pltpu.make_async_copy(
            ints.at[:, pl.ds(first, width)], x.at[:, pl.ds(first - base, width)], sems.at[j]
        )
        for j, (first, width) in enumerate(spans)
    ]
    if q0 + nq < GRP:
        wide = min(HEAD, EDGE - start_of(q0 + nq))
        copies.append(pltpu.make_async_copy(ints.at[:, pl.ds(start_of(q0 + nq), wide)], refs[3].at[:, pl.ds(0, wide)], sems.at[nq // 2 - 1]))
    for c in copies:
        c.start()
    if q0 + nq == GRP and nq > 2:
        x[:, EDGE - base : EDGE - base + 128] = tail[...]
    for b in (ba, bb):
        b[ABD - 8 : ABP, :] = jnp.zeros((ABP - ABD + 8, SPAN), BF)
        b[ABP + ABD - 8 : 2 * ABP, :] = jnp.zeros((ABP - ABD + 8, SPAN), BF)
    row = lax.broadcasted_iota(I32, (128, WIN), 0)
    lane = lax.broadcasted_iota(I32, (2 * ABP, 128), 1)
    turned = jnp.where(lane < 62, lane + 63, lane - 62).astype(F32).astype(BF)
    lane = lane.astype(F32).astype(BF)

    def load(i, b):
        begin = start_of(q0 + i) - start_of(q0 + i // 2 * 2 if i < 2 else q0 + 2)
        w = (head if i < 2 else x)[:, begin : begin + SPAN]
        if q0 + i == GRP - 1 and i < 2:
            w = jnp.concatenate([w[:, : SPAN - 128], tail[...]], axis=1)
        hi, lo = split(w)
        b[0:ABD, :] = hi
        b[ABP : ABP + ABD, :] = lo

    def sort(i, e, b, m):
        start = NV * 5 * (q0 + i)
        at = start - start // 128 * 128 + NV * e
        first = at // 128 * 128
        v = (5 * (q0 + i) + e) % 8
        rank = aux[v, 0:8, :]
        irrep = aux[v, 8:16, :]
        inside = rank >= 0
        sector = jnp.bitwise_xor(irrep, virt_s[c0 + 5 * (q0 + i) + e])
        place = rank + 50 * e
        place = jnp.where(place >= 125, place - 125, place)
        place = place + 62 * jnp.bitwise_and(sector, 1)
        place = jnp.where(place >= 125, place - 125, place)
        place = jnp.where(inside, place, -1)
        pick = jnp.where(jnp.broadcast_to(place[0:1, :], (128, WIN)) == row, 1.0, 0.0).astype(BF)
        half = jnp.where(inside, lax.shift_right_logical(sector, 1), -1)
        for u in range(4):
            on = jnp.where(half[0:1, :] == u, 1.0, 0.0).astype(BF)
            m[e, 128 * u : 128 * u + 128, :] = pick * jnp.broadcast_to(on, (128, WIN))
        return nt(b[:, first : first + WIN], m[e]).astype(BF)

    def merge(i, u, parts):
        to = 256 * i
        r = [p[:, 128 * u : 128 * u + 128] for p in parts]
        for odd in range(2):
            at = turned if odd else lane
            for t in range(2):
                edges = [(50, r[0]), (100, r[1]), (128, r[2])] if t == 0 else [(25, r[2]), (75, r[3]), (128, r[4])]
                y = where_in_lanes(at, edges)
                lhi[2 * u + odd, :, to + 128 * t : to + 128 * t + 128] = y[0:ABP]
                llo[2 * u + odd, :, to + 128 * t : to + 128 * t + 128] = y[ABP : 2 * ABP]

    def pair(k):
        i = 2 * k
        if k:
            copies[k - 1].wait()
        load(i, ba)
        load(i + 1, bb)
        pa = [sort(i, e, ba, ma) for e in range(5)]
        pb = []
        for e in range(5):
            pb.append(sort(i + 1, e, bb, mb))
            if e < 4:
                merge(i, e, pa)
        for u in range(4):
            merge(i + 1, u, pb)

    for k in range(nq // 2):
        pair(k)
    for c in copies[nq // 2 - 1 :]:
        c.wait()
    done[...] = jnp.zeros_like(done)


def main_kernel(rows, widths, *refs):
    n = len(widths)
    pieces = refs[:8]
    ls = refs[8 : 8 + 2 * n]
    out, ghi, glo, acc, pair, order = refs[8 + 3 * n :]
    for j in range(8):
        x = pieces[j][...]
        hi, lo = split(x)
        ghi[32 * j : 32 * j + 32, :] = hi
        glo[32 * j : 32 * j + 32, :] = lo
    last = jnp.concatenate([p[:, PAY - 128 : PAY] for p in pieces], axis=0)
    pair[...] = jnp.transpose(last)[120:128, :]
    acc[...] = jnp.zeros_like(acc)

    def some(step, carry):
        total = None
        k = 0
        for i, w in enumerate(widths):
            hi = ls[2 * i][pl.ds(SECT * step, SECT)].reshape(SECT * ABP, w)
            lo = ls[2 * i + 1][pl.ds(SECT * step, SECT)].reshape(SECT * ABP, w)
            x = nt(hi, ghi[:, k : k + w]) + nt(lo, ghi[:, k : k + w]) + nt(hi, glo[:, k : k + w])
            total = x if total is None else total + x
            k += w
        part = acc[...]
        for i in range(SECT):
            own = jnp.broadcast_to(pair[7:8, :], (ABP, OP)) == (SECT * step + i).astype(F32)
            part = part + jnp.where(own, total[ABP * i : ABP * i + ABP, :], 0.0)
        acc[...] = part
        return carry

    lax.fori_loop(0, NI // SECT, some, 0)
    t = jnp.transpose(acc[...])
    me = rows()
    core, y, x = lax.rem(me, 2), lax.rem(me // 2, 4), me // 8
    for j in range(8):
        kind = core if j < 4 else 1 - core
        for i in range(4):
            d1, d2 = HOPS[i], HOPS[j % 4]
            dx = jnp.where(kind == 0, d1, d2)
            dy = jnp.where(kind == 0, d2, d1)
            shard = (lax.rem(x + 4 - dx, 4) * 4 + lax.rem(y + 4 - dy, 4)) * 2 + kind
            to = pl.multiple_of(shard * OJ, OJ)
            order[pl.ds(to, OJ), :] = t[32 * j + 8 * i : 32 * j + 8 * i + 8, :]
    for b in range(8):
        out[b, 0:32, :] = order[32 * b : 32 * b + 32, 0:128]
        rest = [order[32 * b + 8 * g : 32 * b + 8 * g + 8, 128:ABP] for g in range(4)]
        out[b, 32:40, :] = jnp.concatenate(rest, axis=1)


def finish(got, resid):
    total = jnp.sum(got, axis=0)
    rest = [total[32:40, 32 * g : 32 * g + ABD - 128] for g in range(4)]
    return resid + jnp.concatenate([total[0:32], jnp.concatenate(rest, axis=0)], axis=1)


def smem():
    return pl.BlockSpec(memory_space=pltpu.SMEM)


def in_hbm(x):
    return pltpu.with_memory_space_constraint(x, pltpu.HBM)


def whole(shape):
    return pl.BlockSpec(shape, lambda g: (0,) * len(shape))


def compact(blk, virt, pair, amp, ints):
    hbm = pl.BlockSpec(memory_space=pltpu.HBM)
    return pl.pallas_call(
        functools.partial(compact_kernel, blk),
        out_shape=(
            jax.ShapeDtypeStruct((OJ, PAY), F32),
            jax.ShapeDtypeStruct((4 * OJ, PAY), F32),
            pltpu.VMEM((8, 16, WIN), I32),
            pltpu.VMEM((ABD, 128), F32),
            pltpu.VMEM((ABD, HEAD), F32),
        ),
        grid=(1,),
        in_specs=[
            smem(),
            smem(),
            whole((1, NV)),
            hbm,
            hbm,
            pl.BlockSpec((ABD, 128), lambda g: (0, EDGE // 128)),
        ],
        out_specs=(
            pl.BlockSpec(memory_space=pl.ANY),
            pl.BlockSpec(memory_space=pl.ANY),
            whole((8, 16, WIN)),
            whole((ABD, 128)),
            pl.BlockSpec(memory_space=pl.ANY),
        ),
        scratch_shapes=[pltpu.VMEM((OJ, CD), F32), pltpu.VMEM((OJ, PAY), F32), pltpu.SemaphoreType.DMA((4,))],
        compiler_params=pltpu.CompilerParams(vmem_limit_bytes=COMPACT_VMEM),
        name="compact",
    )(virt, pair, virt.reshape(1, NV), in_hbm(amp), in_hbm(ints), in_hbm(ints))


def sort_part(blk, q0, nq, virt, aux, tail, head, ints):
    shape = pltpu.VMEM((NI, ABP, 256 * nq), BF)
    vmem = pl.BlockSpec(memory_space=pltpu.VMEM)
    more = q0 + nq < GRP
    return pl.pallas_call(
        functools.partial(sort_kernel, blk, q0, nq),
        out_shape=(shape, shape, pltpu.VMEM((8, 128), F32)) + (pltpu.VMEM((ABD, HEAD), F32),) * more,
        in_specs=[smem(), vmem, vmem, vmem, pl.BlockSpec(memory_space=pltpu.HBM)],
        out_specs=(vmem,) * (3 + more),
        scratch_shapes=[
            pltpu.VMEM((ABD, max(start_of(q0 + nq - 1) + SPAN - start_of(q0 + 2), 128)), F32),
            pltpu.VMEM((2 * ABP, SPAN), BF),
            pltpu.VMEM((2 * ABP, SPAN), BF),
            pltpu.VMEM((5, 512, WIN), BF),
            pltpu.VMEM((5, 512, WIN), BF),
            pltpu.SemaphoreType.DMA((nq // 2,)),
        ],
        compiler_params=pltpu.CompilerParams(vmem_limit_bytes=SORT_VMEM),
        cost_estimate=pl.CostEstimate(flops=nq * 5 * 2 * 320 * 512 * 512, bytes_accessed=nq * 1300000, transcendentals=0),
        name="sort_ints",
    )(virt, aux, tail, head, in_hbm(ints))


def contract(rows, pieces, parts):
    widths = tuple(p[0].shape[2] for p in parts)
    flat = [x for p in parts for x in p[:2]]
    vmem = pl.BlockSpec(memory_space=pltpu.VMEM)
    hbm = pl.BlockSpec(memory_space=pl.ANY)
    return pl.pallas_call(
        functools.partial(main_kernel, rows, widths),
        out_shape=jax.ShapeDtypeStruct((8, 40, 128), F32),
        in_specs=[vmem] * (8 + len(flat)) + [hbm] * len(parts),
        out_specs=vmem,
        scratch_shapes=[
            pltpu.VMEM((OP, PAY), BF),
            pltpu.VMEM((OP, PAY), BF),
            pltpu.VMEM((ABP, OP), F32),
            pltpu.VMEM((8, OP), F32),
            pltpu.VMEM((OP, ABP), F32),
        ],
        compiler_params=pltpu.CompilerParams(vmem_limit_bytes=VMEM_LIMIT),
        cost_estimate=pl.CostEstimate(flops=3 * 2 * 1280 * 2560 * 256, bytes_accessed=16000000, transcendentals=0),
        name="contract",
    )(*pieces, *[pltpu.with_memory_space_constraint(x, pltpu.VMEM) for x in flat], *[p[2] for p in parts])


def at(x, y, core):
    return ((x % 4) * 4 + y % 4) * 2 + core


def walk(hop, second):
    pairs = []
    for x in range(4):
        for y in range(4):
            for core in range(2):
                along_x = (core == 0) != second
                to = at(x + hop, y, core) if along_x else at(x, y + hop, core)
                pairs.append((at(x, y, core), to))
    return pairs


SWAP = [(i, i ^ 1) for i in range(32)]


def body(amplitudes, pair_irrep, virt_irrep, resid_in, ladder_ints):
    blk = functools.partial(lax.axis_index, "blk")
    hold = lax.optimization_barrier
    pay, four, aux, tail, head = compact(blk, virt_irrep, pair_irrep, amplitudes, ladder_ints)

    def sort(q0, nq, aux, head):
        return list(sort_part(blk, q0, nq, virt_irrep, aux, tail, head, ladder_ints))

    line = [lax.ppermute(pay, "rows", walk(h, False)) for h in HOPS[1:]]
    parts = [sort(*PARTS[0], aux, head)]
    line, parts[0][2], aux = hold((line, parts[0][2], aux))
    for i, x in enumerate(line):
        four = lax.dynamic_update_slice(four, x, (OJ * (i + 1), 0))
    near = [lax.ppermute(four, "rows", walk(h, True)) for h in HOPS[1:]]
    far = [lax.ppermute(four, "rows", SWAP)]
    parts.append(sort(*PARTS[1], aux, parts[0][3]))
    near, parts[1][2], aux = hold((near, parts[1][2], aux))
    far += [lax.ppermute(p, "rows", SWAP) for p in near]
    parts.append(sort(*PARTS[2], aux, parts[1][3]))
    terms = contract(functools.partial(lax.axis_index, "rows"), [four] + near + far, parts)
    return finish(lax.all_to_all(terms, "blk", 0, 0), resid_in)


def solution(mesh):
    placed = (P("rows", "blk"), P("rows"), P(), P("blk", "rows"), P("rows", "blk"))
    return jax.shard_map(
        body, mesh=mesh, in_specs=placed, out_specs=P("blk", "rows"), check_vma=False
    )
```

```python
import functools

import jax
import jax.numpy as jnp
from jax import lax
from jax.experimental import pallas as pl
from jax.experimental.pallas import tpu as pltpu
from jax.sharding import PartitionSpec as P

BF = jnp.bfloat16
F32 = jnp.float32
I32 = jnp.int32

NV = 400
NI = 8
PER = 50
CN = 50
WIN = 512
OJ = 8
OP = 256
ABD = 152
ABP = 160
ABS = 2 * ABD
PAY = 2560
GRP = 10
SPAN = 2176
HEAD = 4224
CD = CN * NV
EDGE = CD // 128 * 128
HOPS = (0, 2, 1, 3)
PARTS = ((0, 2), (2, 6), (8, 2))
SECT = 4
VMEM_LIMIT = 24 * 1024 * 1024
COMPACT_VMEM = 56 * 1024 * 1024
SORT_VMEM = 22 * 1024 * 1024


def nt(a, b):
    return lax.dot_general(a, b, (((1,), (1,)), ((), ())), preferred_element_type=F32)


def split(x):
    hi = x.astype(BF)
    return hi, (x - hi.astype(F32)).astype(BF)


def where_in_lanes(lane, pieces):
    out = pieces[-1][1]
    for edge, x in reversed(pieces[:-1]):
        out = jnp.where(lane < edge, x, out)
    return out


def turn(lane, x):
    moved = jnp.where(lane < 62, pltpu.roll(x, 65, 1), pltpu.roll(x, 62, 1))
    return jnp.where(lane < 125, moved, 0.0)


def compact_kernel(blk, virt_s, pair_s, virt_v, amp, edge, pays, four, aux, tail, pay, sems):
    c0 = blk() * CN
    lane = lax.broadcasted_iota(I32, (8, WIN), 1)
    sub = lax.broadcasted_iota(I32, (8, WIN), 0)
    irrep = jnp.concatenate([virt_v[...], jnp.full((1, WIN - NV), -1, I32)], axis=1)
    irrep = jnp.broadcast_to(irrep, (8, WIN))
    member = irrep == sub
    before = lax.broadcasted_iota(I32, (WIN, WIN), 0) < lax.broadcasted_iota(I32, (WIN, WIN), 1)
    count = jnp.dot(
        jnp.where(member, 1.0, 0.0).astype(BF),
        jnp.where(before, 1.0, 0.0).astype(BF),
        preferred_element_type=F32,
    )
    rank = jnp.sum(jnp.where(member, count, 0.0), axis=0, keepdims=True).astype(I32)
    rank = jnp.where(lane < NV, jnp.broadcast_to(rank, (8, WIN)), -1)
    tail[...] = jnp.where(lax.broadcasted_iota(I32, (ABD, 128), 1) < CD - EDGE, edge[...], 0.0)
    pair = jnp.zeros((8, WIN), I32)
    for i in range(OJ):
        pair = jnp.where(sub == i, pair_s[i], pair)
    need = jnp.where(lane < NV, jnp.bitwise_xor(irrep, pair), -1)
    row = lax.broadcasted_iota(I32, (128, WIN), 0)
    rows = {}
    for v in range(8):
        need_v = pltpu.roll(need, 16 * v, 1) if v else need
        rank_v = pltpu.roll(rank, 16 * v, 1) if v else rank
        aux[v, 0:8, :] = rank_v
        aux[v, 8:16, :] = pltpu.roll(irrep, 16 * v, 1) if v else irrep
        pick = jnp.where(jnp.broadcast_to(rank_v[0:1, :], (128, WIN)) == row, 1.0, 0.0).astype(BF)
        cs = list(range(v, CN, 8))
        xs = []
        for c in cs:
            first = (NV * c) // 128 * 128
            width = min(WIN, CD - first)
            x = amp[:, first : first + width]
            if width < WIN:
                x = jnp.concatenate([x, jnp.zeros((8, WIN - width), F32)], axis=1)
            xs.append(jnp.where(need_v == virt_s[c0 + c], x, 0.0))
        if len(xs) % 2:
            xs.append(jnp.zeros((8, WIN), F32))
        hi, lo = split(jnp.concatenate(xs, axis=0))
        r = nt(hi, pick) + nt(lo, pick)
        for i, c in enumerate(cs):
            rows[c] = r[8 * i : 8 * i + 8, :]
    lane = lax.broadcasted_iota(I32, (8, 128), 1)
    odd = jnp.bitwise_and(pair[:, 0:128], 1) == 1
    for q in range(GRP):
        r0, r1, r2, r3, r4 = (rows[5 * q + e] for e in range(5))
        r1 = pltpu.roll(r1, 50, 1)
        r2a = pltpu.roll(r2, 100, 1)
        r2b = pltpu.roll(r2, 103, 1)
        r3 = pltpu.roll(r3, 25, 1)
        r4 = pltpu.roll(r4, 75, 1)
        a = where_in_lanes(lane, [(50, r0), (100, r1), (125, r2a), (128, jnp.zeros_like(r0))])
        b = where_in_lanes(lane, [(25, r2b), (75, r3), (128, r4)])
        a = jnp.where(odd, turn(lane, a), a)
        b = jnp.where(odd, turn(lane, b), b)
        if q == GRP - 1:
            b = jnp.where(lane == 127, pair[:, 0:128].astype(F32), b)
        pay[:, 256 * q : 256 * q + 128] = a
        pay[:, 256 * q + 128 : 256 * q + 256] = b
    copies = [
        pltpu.make_async_copy(pay, pays, sems.at[0]),
        pltpu.make_async_copy(pay, four.at[pl.ds(0, OJ), :], sems.at[1]),
    ]
    for c in copies:
        c.start()
    for c in copies:
        c.wait()


def start_of(q):
    return NV * 5 * q // 128 * 128


def chunks(q0, nq):
    edges = [start_of(q0 + 2)] + [min(start_of(q) + SPAN, EDGE) for q in range(q0 + 3, q0 + nq, 2)]
    return [(a, b - a) for a, b in zip(edges, edges[1:])]


def sort_kernel(blk, q0, nq, virt_s, aux, tail, ints, *refs):
    if q0:
        head, *refs = refs
    else:
        *refs, head, head_sems = refs
    both, done = refs[:2]
    x, ba, bb, ma, mb, sems = refs[-6:]
    c0 = blk() * CN
    spans = chunks(q0, nq)
    base = start_of(q0 + 2)
    copies = [
        pltpu.make_async_copy(
            ints.at[:, pl.ds(first, width)], x.at[:, pl.ds(first - base, width)], sems.at[j]
        )
        for j, (first, width) in enumerate(spans)
    ]
    if q0 + nq < GRP:
        wide = min(HEAD, EDGE - start_of(q0 + nq))
        copies.append(pltpu.make_async_copy(ints.at[:, pl.ds(start_of(q0 + nq), wide)], refs[2].at[:, pl.ds(0, wide)], sems.at[nq // 2 - 1]))
    first = []
    if not q0:
        first = [
            pltpu.make_async_copy(ints.at[:, pl.ds(a, w)], head.at[:, pl.ds(a, w)], head_sems.at[j])
            for j, (a, w) in enumerate(((0, SPAN), (SPAN, HEAD - SPAN)))
        ]
    for c in first + copies:
        c.start()
    if q0 + nq == GRP and nq > 2:
        x[:, EDGE - base : EDGE - base + 128] = tail[...]
    row = lax.broadcasted_iota(I32, (128, WIN), 0)
    lane = lax.broadcasted_iota(I32, (ABS, 128), 1)
    turned = jnp.where(lane < 62, lane + 63, lane - 62).astype(F32).astype(BF)
    lane = lane.astype(F32).astype(BF)

    def load(i, b):
        begin = start_of(q0 + i) - start_of(q0 + i // 2 * 2 if i < 2 else q0 + 2)
        w = (head if i < 2 else x)[:, begin : begin + SPAN]
        if q0 + i == GRP - 1 and i < 2:
            w = jnp.concatenate([w[:, : SPAN - 128], tail[...]], axis=1)
        hi = w.astype(BF).astype(F32)
        b[...] = jnp.concatenate([hi, w - hi], axis=0).astype(BF)

    def sort(i, e, b, m):
        start = NV * 5 * (q0 + i)
        at = start - start // 128 * 128 + NV * e
        first = at // 128 * 128
        v = (5 * (q0 + i) + e) % 8
        rank = aux[v, 0:8, :]
        irrep = aux[v, 8:16, :]
        inside = rank >= 0
        sector = jnp.bitwise_xor(irrep, virt_s[c0 + 5 * (q0 + i) + e])
        place = rank + 50 * e
        place = jnp.where(place >= 125, place - 125, place)
        place = place + 62 * jnp.bitwise_and(sector, 1)
        place = jnp.where(place >= 125, place - 125, place)
        place = jnp.where(inside, place, -1)
        pick = jnp.where(jnp.broadcast_to(place[0:1, :], (128, WIN)) == row, 1.0, 0.0).astype(BF)
        half = jnp.where(inside, lax.shift_right_logical(sector, 1), -1)
        for u in range(4):
            on = jnp.where(half[0:1, :] == u, 1.0, 0.0).astype(BF)
            m[e, 128 * u : 128 * u + 128, :] = pick * jnp.broadcast_to(on, (128, WIN))
        return nt(b[:, first : first + WIN], m[e]).astype(BF)

    def merge(i, u, parts):
        to = 256 * i
        r = [p[:, 128 * u : 128 * u + 128] for p in parts]
        for odd in range(2):
            at = turned if odd else lane
            for t in range(2):
                edges = [(50, r[0]), (100, r[1]), (128, r[2])] if t == 0 else [(25, r[2]), (75, r[3]), (128, r[4])]
                y = where_in_lanes(at, edges)
                both[2 * u + odd, :, to + 128 * t : to + 128 * t + 128] = y

    def pair(k):
        i = 2 * k
        if k:
            copies[k - 1].wait()
        if first and not k:
            first[0].wait()
            load(i, ba)
            pa = [sort(i, e, ba, ma) for e in range(2)]
            first[1].wait()
            load(i + 1, bb)
            pa += [sort(i, e, ba, ma) for e in range(2, 5)]
        else:
            load(i, ba)
            load(i + 1, bb)
            pa = [sort(i, e, ba, ma) for e in range(5)]
        pb = []
        for e in range(5):
            pb.append(sort(i + 1, e, bb, mb))
            if e < 4:
                merge(i, e, pa)
        for u in range(4):
            merge(i + 1, u, pb)

    for k in range(nq // 2):
        pair(k)
    for c in copies[nq // 2 - 1 :]:
        c.wait()
    done[...] = jnp.zeros_like(done)


def main_kernel(rows, widths, *refs):
    n = len(widths)
    pieces = refs[:8]
    ls = refs[8 : 8 + n]
    out, ghi, glo, acc, pair, order = refs[8 + 2 * n :]
    for j in range(8):
        x = pieces[j][...]
        hi, lo = split(x)
        ghi[32 * j : 32 * j + 32, :] = hi
        glo[32 * j : 32 * j + 32, :] = lo
    last = jnp.concatenate([p[:, PAY - 128 : PAY] for p in pieces], axis=0)
    pair[...] = jnp.transpose(last)[120:128, :]
    acc[...] = jnp.zeros_like(acc)

    def some(step, carry):
        total = None
        k = 0
        for i, w in enumerate(widths):
            both = ls[i][pl.ds(SECT * step, SECT)]
            x = nt(both.reshape(SECT * ABS, w), ghi[:, k : k + w])
            y = nt(both[:, 0:ABP].reshape(SECT * ABP, w), glo[:, k : k + w])
            total = (x, y) if total is None else (total[0] + x, total[1] + y)
            k += w
        part = acc[...]
        for i in range(SECT):
            x, y = total[0][ABS * i : ABS * i + ABS], total[1][ABP * i : ABP * i + ABD]
            own = jnp.broadcast_to(pair[7:8, :], (ABD, OP)) == (SECT * step + i).astype(F32)
            part = part + jnp.where(own, x[0:ABD] + x[ABD:ABS] + y, 0.0)
        acc[...] = part
        return carry

    lax.fori_loop(0, NI // SECT, some, 0)
    t = jnp.transpose(jnp.concatenate([acc[...], jnp.zeros((ABP - ABD, OP), F32)], axis=0))
    me = rows()
    core, y, x = lax.rem(me, 2), lax.rem(me // 2, 4), me // 8
    for j in range(8):
        kind = core if j < 4 else 1 - core
        for i in range(4):
            d1, d2 = HOPS[i], HOPS[j % 4]
            dx = jnp.where(kind == 0, d1, d2)
            dy = jnp.where(kind == 0, d2, d1)
            shard = (lax.rem(x + 4 - dx, 4) * 4 + lax.rem(y + 4 - dy, 4)) * 2 + kind
            to = pl.multiple_of(shard * OJ, OJ)
            order[pl.ds(to, OJ), :] = t[32 * j + 8 * i : 32 * j + 8 * i + 8, :]
    for b in range(8):
        out[b, 0:32, :] = order[32 * b : 32 * b + 32, 0:128]
        rest = [order[32 * b + 8 * g : 32 * b + 8 * g + 8, 128:ABP] for g in range(4)]
        out[b, 32:40, :] = jnp.concatenate(rest, axis=1)


def finish(got, resid):
    total = jnp.sum(got, axis=0)
    rest = [total[32:40, 32 * g : 32 * g + ABD - 128] for g in range(4)]
    return resid + jnp.concatenate([total[0:32], jnp.concatenate(rest, axis=0)], axis=1)


def smem():
    return pl.BlockSpec(memory_space=pltpu.SMEM)


def in_hbm(x):
    return pltpu.with_memory_space_constraint(x, pltpu.HBM)


def whole(shape):
    return pl.BlockSpec(shape, lambda g: (0,) * len(shape))


def compact(blk, virt, pair, amp, ints):
    return pl.pallas_call(
        functools.partial(compact_kernel, blk),
        out_shape=(
            pltpu.VMEM((OJ, PAY), F32),
            pltpu.VMEM((4 * OJ, PAY), F32),
            pltpu.VMEM((8, 16, WIN), I32),
            pltpu.VMEM((ABD, 128), F32),
        ),
        grid=(1,),
        in_specs=[
            smem(),
            smem(),
            whole((1, NV)),
            whole((OJ, CD)),
            pl.BlockSpec((ABD, 128), lambda g: (0, EDGE // 128)),
        ],
        out_specs=(
            pl.BlockSpec(memory_space=pl.ANY),
            pl.BlockSpec(memory_space=pl.ANY),
            whole((8, 16, WIN)),
            whole((ABD, 128)),
        ),
        scratch_shapes=[pltpu.VMEM((OJ, PAY), F32), pltpu.SemaphoreType.DMA((2,))],
        compiler_params=pltpu.CompilerParams(vmem_limit_bytes=COMPACT_VMEM),
        name="compact",
    )(virt, pair, virt.reshape(1, NV), in_hbm(amp), in_hbm(ints))


def sort_part(blk, q0, nq, virt, aux, tail, head, ints):
    shape = pltpu.VMEM((NI, ABS, 256 * nq), BF)
    vmem = pl.BlockSpec(memory_space=pltpu.VMEM)
    more = q0 + nq < GRP
    heads = [head] if q0 else []
    return pl.pallas_call(
        functools.partial(sort_kernel, blk, q0, nq),
        out_shape=(shape, pltpu.VMEM((8, 128), F32)) + (pltpu.VMEM((ABD, HEAD), F32),) * more,
        in_specs=[smem(), vmem, vmem, pl.BlockSpec(memory_space=pltpu.HBM)] + [vmem] * len(heads),
        out_specs=(vmem,) * (2 + more),
        scratch_shapes=[
            pltpu.VMEM((ABD, max(start_of(q0 + nq - 1) + SPAN - start_of(q0 + 2), 128)), F32),
            pltpu.VMEM((ABS, SPAN), BF),
            pltpu.VMEM((ABS, SPAN), BF),
            pltpu.VMEM((5, 512, WIN), BF),
            pltpu.VMEM((5, 512, WIN), BF),
            pltpu.SemaphoreType.DMA((nq // 2,)),
        ]
        + [pltpu.VMEM((ABD, HEAD), F32), pltpu.SemaphoreType.DMA((2,))] * (not q0),
        compiler_params=pltpu.CompilerParams(vmem_limit_bytes=SORT_VMEM),
        cost_estimate=pl.CostEstimate(flops=nq * 5 * 2 * ABS * 512 * 512, bytes_accessed=nq * 1300000, transcendentals=0),
        name="sort_ints",
    )(virt, aux, tail, in_hbm(ints), *heads)


def contract(rows, pieces, parts):
    widths = tuple(p[0].shape[2] for p in parts)
    flat = [p[0] for p in parts]
    vmem = pl.BlockSpec(memory_space=pltpu.VMEM)
    hbm = pl.BlockSpec(memory_space=pl.ANY)
    return pl.pallas_call(
        functools.partial(main_kernel, rows, widths),
        out_shape=jax.ShapeDtypeStruct((8, 40, 128), F32),
        in_specs=[vmem] * (8 + len(flat)) + [hbm] * len(parts),
        out_specs=vmem,
        scratch_shapes=[
            pltpu.VMEM((OP, PAY), BF),
            pltpu.VMEM((OP, PAY), BF),
            pltpu.VMEM((ABD, OP), F32),
            pltpu.VMEM((8, OP), F32),
            pltpu.VMEM((OP, ABP), F32),
        ],
        compiler_params=pltpu.CompilerParams(vmem_limit_bytes=VMEM_LIMIT),
        cost_estimate=pl.CostEstimate(flops=3 * 2 * 1280 * 2560 * 256, bytes_accessed=16000000, transcendentals=0),
        name="contract",
    )(*pieces, *[pltpu.with_memory_space_constraint(x, pltpu.VMEM) for x in flat], *[p[1] for p in parts])


def at(x, y, core):
    return ((x % 4) * 4 + y % 4) * 2 + core


def walk(hop, second):
    pairs = []
    for x in range(4):
        for y in range(4):
            for core in range(2):
                along_x = (core == 0) != second
                to = at(x + hop, y, core) if along_x else at(x, y + hop, core)
                pairs.append((at(x, y, core), to))
    return pairs


SWAP = [(i, i ^ 1) for i in range(32)]


def body(amplitudes, pair_irrep, virt_irrep, resid_in, ladder_ints):
    blk = functools.partial(lax.axis_index, "blk")
    hold = lax.optimization_barrier
    pay, four, aux, tail = compact(blk, virt_irrep, pair_irrep, amplitudes, ladder_ints)

    def sort(q0, nq, aux, head=None):
        return list(sort_part(blk, q0, nq, virt_irrep, aux, tail, head, ladder_ints))

    line = [lax.ppermute(pay, "rows", walk(h, False)) for h in HOPS[1:]]
    parts = [sort(*PARTS[0], aux)]
    line, parts[0][1], aux = hold((line, parts[0][1], aux))
    for i, x in enumerate(line):
        four = lax.dynamic_update_slice(four, x, (OJ * (i + 1), 0))
    near = [lax.ppermute(four, "rows", walk(h, True)) for h in HOPS[1:]]
    far = [lax.ppermute(four, "rows", SWAP)]
    parts.append(sort(*PARTS[1], aux, parts[0][2]))
    near, parts[1][1], aux = hold((near, parts[1][1], aux))
    far += [lax.ppermute(p, "rows", SWAP) for p in near]
    parts.append(sort(*PARTS[2], aux, parts[1][2]))
    terms = contract(functools.partial(lax.axis_index, "rows"), [four] + near + far, parts)
    return finish(lax.all_to_all(terms, "blk", 0, 0), resid_in)


def solution(mesh):
    placed = (P("rows", "blk"), P("rows"), P(), P("blk", "rows"), P("rows", "blk"))
    return jax.shard_map(
        body, mesh=mesh, in_specs=placed, out_specs=P("blk", "rows"), check_vma=False
    )
```

```python
import functools

import jax
import jax.numpy as jnp
from jax import lax
from jax.experimental import pallas as pl
from jax.experimental.pallas import tpu as pltpu
from jax.sharding import PartitionSpec as P

BF = jnp.bfloat16
F32 = jnp.float32
I32 = jnp.int32

NV = 400
NI = 8
PER = 50
CN = 50
WIN = 512
OJ = 8
OP = 256
ABD = 152
ABP = 160
ABS = 2 * ABD
PAY = 2560
GRP = 10
SPAN = 2176
HEAD = 4224
CD = CN * NV
EDGE = CD // 128 * 128
HOPS = (0, 2, 1, 3)
PARTS = ((0, 2), (2, 6), (8, 2))
SECT = 8
VMEM_LIMIT = 24 * 1024 * 1024
COMPACT_VMEM = 56 * 1024 * 1024
SORT_VMEM = 22 * 1024 * 1024


def nt(a, b):
    return lax.dot_general(a, b, (((1,), (1,)), ((), ())), preferred_element_type=F32)


def split(x):
    hi = x.astype(BF)
    return hi, (x - hi.astype(F32)).astype(BF)


def where_in_lanes(lane, pieces):
    out = pieces[-1][1]
    for edge, x in reversed(pieces[:-1]):
        out = jnp.where(lane < edge, x, out)
    return out


def turn(lane, x):
    moved = jnp.where(lane < 62, pltpu.roll(x, 65, 1), pltpu.roll(x, 62, 1))
    return jnp.where(lane < 125, moved, 0.0)


def compact_kernel(blk, virt_s, pair_s, virt_v, amp, edge, pays, four, aux, tail, pay, sems):
    c0 = blk() * CN
    lane = lax.broadcasted_iota(I32, (8, WIN), 1)
    sub = lax.broadcasted_iota(I32, (8, WIN), 0)
    irrep = jnp.concatenate([virt_v[...], jnp.full((1, WIN - NV), -1, I32)], axis=1)
    irrep = jnp.broadcast_to(irrep, (8, WIN))
    member = irrep == sub
    before = lax.broadcasted_iota(I32, (WIN, WIN), 0) < lax.broadcasted_iota(I32, (WIN, WIN), 1)
    count = jnp.dot(
        jnp.where(member, 1.0, 0.0).astype(BF),
        jnp.where(before, 1.0, 0.0).astype(BF),
        preferred_element_type=F32,
    )
    rank = jnp.sum(jnp.where(member, count, 0.0), axis=0, keepdims=True).astype(I32)
    rank = jnp.where(lane < NV, jnp.broadcast_to(rank, (8, WIN)), -1)
    tail[...] = jnp.where(lax.broadcasted_iota(I32, (ABD, 128), 1) < CD - EDGE, edge[...], 0.0)
    pair = jnp.zeros((8, WIN), I32)
    for i in range(OJ):
        pair = jnp.where(sub == i, pair_s[i], pair)
    need = jnp.where(lane < NV, jnp.bitwise_xor(irrep, pair), -1)
    row = lax.broadcasted_iota(I32, (128, WIN), 0)
    rows = {}
    for v in range(8):
        need_v = pltpu.roll(need, 16 * v, 1) if v else need
        rank_v = pltpu.roll(rank, 16 * v, 1) if v else rank
        aux[v, 0:8, :] = rank_v
        aux[v, 8:16, :] = pltpu.roll(irrep, 16 * v, 1) if v else irrep
        pick = jnp.where(jnp.broadcast_to(rank_v[0:1, :], (128, WIN)) == row, 1.0, 0.0).astype(BF)
        cs = list(range(v, CN, 8))
        xs = []
        for c in cs:
            first = (NV * c) // 128 * 128
            width = min(WIN, CD - first)
            x = amp[:, first : first + width]
            if width < WIN:
                x = jnp.concatenate([x, jnp.zeros((8, WIN - width), F32)], axis=1)
            xs.append(jnp.where(need_v == virt_s[c0 + c], x, 0.0))
        if len(xs) % 2:
            xs.append(jnp.zeros((8, WIN), F32))
        hi, lo = split(jnp.concatenate(xs, axis=0))
        r = nt(hi, pick) + nt(lo, pick)
        for i, c in enumerate(cs):
            rows[c] = r[8 * i : 8 * i + 8, :]
    lane = lax.broadcasted_iota(I32, (8, 128), 1)
    odd = jnp.bitwise_and(pair[:, 0:128], 1) == 1
    for q in range(GRP):
        r0, r1, r2, r3, r4 = (rows[5 * q + e] for e in range(5))
        r1 = pltpu.roll(r1, 50, 1)
        r2a = pltpu.roll(r2, 100, 1)
        r2b = pltpu.roll(r2, 103, 1)
        r3 = pltpu.roll(r3, 25, 1)
        r4 = pltpu.roll(r4, 75, 1)
        a = where_in_lanes(lane, [(50, r0), (100, r1), (125, r2a), (128, jnp.zeros_like(r0))])
        b = where_in_lanes(lane, [(25, r2b), (75, r3), (128, r4)])
        a = jnp.where(odd, turn(lane, a), a)
        b = jnp.where(odd, turn(lane, b), b)
        if q == GRP - 1:
            b = jnp.where(lane == 127, pair[:, 0:128].astype(F32), b)
        pay[:, 256 * q : 256 * q + 128] = a
        pay[:, 256 * q + 128 : 256 * q + 256] = b
    copies = [
        pltpu.make_async_copy(pay, pays, sems.at[0]),
        pltpu.make_async_copy(pay, four.at[pl.ds(0, OJ), :], sems.at[1]),
    ]
    for c in copies:
        c.start()
    for c in copies:
        c.wait()


def start_of(q):
    return NV * 5 * q // 128 * 128


def chunks(q0, nq):
    edges = [start_of(q0 + 2)] + [min(start_of(q) + SPAN, EDGE) for q in range(q0 + 3, q0 + nq, 2)]
    return [(a, b - a) for a, b in zip(edges, edges[1:])]


def sort_kernel(blk, q0, nq, virt_s, aux, tail, ints, *refs):
    if q0:
        head, *refs = refs
    else:
        *refs, head, head_sems = refs
    both, done = refs[:2]
    x, ba, bb, ma, mb, sems = refs[-6:]
    c0 = blk() * CN
    spans = chunks(q0, nq)
    base = start_of(q0 + 2)
    copies = [
        pltpu.make_async_copy(
            ints.at[:, pl.ds(first, width)], x.at[:, pl.ds(first - base, width)], sems.at[j]
        )
        for j, (first, width) in enumerate(spans)
    ]
    if q0 + nq < GRP:
        wide = min(HEAD, EDGE - start_of(q0 + nq))
        copies.append(pltpu.make_async_copy(ints.at[:, pl.ds(start_of(q0 + nq), wide)], refs[2].at[:, pl.ds(0, wide)], sems.at[nq // 2 - 1]))
    first = []
    if not q0:
        first = [
            pltpu.make_async_copy(ints.at[:, pl.ds(a, w)], head.at[:, pl.ds(a, w)], head_sems.at[j])
            for j, (a, w) in enumerate(((0, SPAN), (SPAN, HEAD - SPAN)))
        ]
    for c in first + copies:
        c.start()
    if q0 + nq == GRP and nq > 2:
        x[:, EDGE - base : EDGE - base + 128] = tail[...]
    row = lax.broadcasted_iota(I32, (128, WIN), 0)
    lane = lax.broadcasted_iota(I32, (ABS, 128), 1)
    turned = jnp.where(lane < 62, lane + 63, lane - 62).astype(F32).astype(BF)
    lane = lane.astype(F32).astype(BF)

    def load(i, b):
        begin = start_of(q0 + i) - start_of(q0 + i // 2 * 2 if i < 2 else q0 + 2)
        w = (head if i < 2 else x)[:, begin : begin + SPAN]
        if q0 + i == GRP - 1 and i < 2:
            w = jnp.concatenate([w[:, : SPAN - 128], tail[...]], axis=1)
        hi = w.astype(BF).astype(F32)
        b[...] = jnp.concatenate([hi, w - hi], axis=0).astype(BF)

    def build(i, e, m):
        v = (5 * (q0 + i) + e) % 8
        rank = aux[v, 0:8, :]
        irrep = aux[v, 8:16, :]
        inside = rank >= 0
        sector = jnp.bitwise_xor(irrep, virt_s[c0 + 5 * (q0 + i) + e])
        place = rank + 50 * e
        place = jnp.where(place >= 125, place - 125, place)
        place = place + 62 * jnp.bitwise_and(sector, 1)
        place = jnp.where(place >= 125, place - 125, place)
        place = jnp.where(inside, place, -1)
        pick = jnp.where(jnp.broadcast_to(place[0:1, :], (128, WIN)) == row, 1.0, 0.0).astype(BF)
        half = jnp.where(inside, lax.shift_right_logical(sector, 1), -1)
        for u in range(4):
            on = jnp.where(half[0:1, :] == u, 1.0, 0.0).astype(BF)
            m[e, 128 * u : 128 * u + 128, :] = pick * jnp.broadcast_to(on, (128, WIN))

    def sort(i, e, b, m, built=False):
        if not built:
            build(i, e, m)
        at = NV * 5 * (q0 + i) - start_of(q0 + i) + NV * e
        first = at // 128 * 128
        return nt(b[:, first : first + WIN], m[e]).astype(BF)

    def merge(i, u, parts):
        to = 256 * i
        r = [p[:, 128 * u : 128 * u + 128] for p in parts]
        for odd in range(2):
            at = turned if odd else lane
            for t in range(2):
                edges = [(50, r[0]), (100, r[1]), (128, r[2])] if t == 0 else [(25, r[2]), (75, r[3]), (128, r[4])]
                y = where_in_lanes(at, edges)
                both[2 * u + odd, :, to + 128 * t : to + 128 * t + 128] = y

    def pair(k):
        i = 2 * k
        if k:
            copies[k - 1].wait()
        if first and not k:
            for e in range(5):
                build(i, e, ma)
                build(i + 1, e, mb)
            first[0].wait()
            load(i, ba)
            pa = [sort(i, e, ba, ma, True) for e in range(2)]
            first[1].wait()
            load(i + 1, bb)
            pa += [sort(i, e, ba, ma, True) for e in range(2, 5)]
        else:
            load(i, ba)
            load(i + 1, bb)
            pa = [sort(i, e, ba, ma) for e in range(5)]
        pb = []
        for e in range(5):
            pb.append(sort(i + 1, e, bb, mb, bool(first) and not k))
            if e < 4:
                merge(i, e, pa)
        for u in range(4):
            merge(i + 1, u, pb)

    for k in range(nq // 2):
        pair(k)
    for c in copies[nq // 2 - 1 :]:
        c.wait()
    done[...] = jnp.zeros_like(done)


def main_kernel(rows, widths, *refs):
    n = len(widths)
    pieces = refs[:8]
    ls = refs[8 : 8 + n]
    out, ghi, glo, acc, pair, order = refs[8 + 2 * n :]
    for j in range(8):
        x = pieces[j][...]
        hi, lo = split(x)
        ghi[32 * j : 32 * j + 32, :] = hi
        glo[32 * j : 32 * j + 32, :] = lo
    last = jnp.concatenate([p[:, PAY - 128 : PAY] for p in pieces], axis=0)
    pair[...] = jnp.transpose(last)[120:128, :]
    acc[...] = jnp.zeros_like(acc)

    def some(step, carry):
        total = None
        k = 0
        for i, w in enumerate(widths):
            both = ls[i][pl.ds(SECT * step, SECT)]
            x = nt(both.reshape(SECT * ABS, w), ghi[:, k : k + w])
            y = nt(both[:, 0:ABP].reshape(SECT * ABP, w), glo[:, k : k + w])
            total = (x, y) if total is None else (total[0] + x, total[1] + y)
            k += w
        part = acc[...]
        for i in range(SECT):
            x, y = total[0][ABS * i : ABS * i + ABS], total[1][ABP * i : ABP * i + ABD]
            own = jnp.broadcast_to(pair[7:8, :], (ABD, OP)) == (SECT * step + i).astype(F32)
            part = part + jnp.where(own, x[0:ABD] + x[ABD:ABS] + y, 0.0)
        acc[...] = part
        return carry

    lax.fori_loop(0, NI // SECT, some, 0)
    t = jnp.transpose(jnp.concatenate([acc[...], jnp.zeros((ABP - ABD, OP), F32)], axis=0))
    me = rows()
    core, y, x = lax.rem(me, 2), lax.rem(me // 2, 4), me // 8
    for j in range(8):
        kind = core if j < 4 else 1 - core
        for i in range(4):
            d1, d2 = HOPS[i], HOPS[j % 4]
            dx = jnp.where(kind == 0, d1, d2)
            dy = jnp.where(kind == 0, d2, d1)
            shard = (lax.rem(x + 4 - dx, 4) * 4 + lax.rem(y + 4 - dy, 4)) * 2 + kind
            to = pl.multiple_of(shard * OJ, OJ)
            order[pl.ds(to, OJ), :] = t[32 * j + 8 * i : 32 * j + 8 * i + 8, :]
    for b in range(8):
        out[b, 0:32, :] = order[32 * b : 32 * b + 32, 0:128]
        rest = [order[32 * b + 8 * g : 32 * b + 8 * g + 8, 128:ABP] for g in range(4)]
        out[b, 32:40, :] = jnp.concatenate(rest, axis=1)


def finish(got, resid):
    total = jnp.sum(got, axis=0)
    rest = [total[32:40, 32 * g : 32 * g + ABD - 128] for g in range(4)]
    return resid + jnp.concatenate([total[0:32], jnp.concatenate(rest, axis=0)], axis=1)


def smem():
    return pl.BlockSpec(memory_space=pltpu.SMEM)


def in_hbm(x):
    return pltpu.with_memory_space_constraint(x, pltpu.HBM)


def whole(shape):
    return pl.BlockSpec(shape, lambda g: (0,) * len(shape))


def compact(blk, virt, pair, amp, ints):
    return pl.pallas_call(
        functools.partial(compact_kernel, blk),
        out_shape=(
            pltpu.VMEM((OJ, PAY), F32),
            pltpu.VMEM((4 * OJ, PAY), F32),
            pltpu.VMEM((8, 16, WIN), I32),
            pltpu.VMEM((ABD, 128), F32),
        ),
        grid=(1,),
        in_specs=[
            smem(),
            smem(),
            whole((1, NV)),
            whole((OJ, CD)),
            pl.BlockSpec((ABD, 128), lambda g: (0, EDGE // 128)),
        ],
        out_specs=(
            pl.BlockSpec(memory_space=pl.ANY),
            pl.BlockSpec(memory_space=pl.ANY),
            whole((8, 16, WIN)),
            whole((ABD, 128)),
        ),
        scratch_shapes=[pltpu.VMEM((OJ, PAY), F32), pltpu.SemaphoreType.DMA((2,))],
        compiler_params=pltpu.CompilerParams(vmem_limit_bytes=COMPACT_VMEM),
        name="compact",
    )(virt, pair, virt.reshape(1, NV), in_hbm(amp), in_hbm(ints))


def sort_part(blk, q0, nq, virt, aux, tail, head, ints):
    shape = pltpu.VMEM((NI, ABS, 256 * nq), BF)
    vmem = pl.BlockSpec(memory_space=pltpu.VMEM)
    more = q0 + nq < GRP
    heads = [head] if q0 else []
    return pl.pallas_call(
        functools.partial(sort_kernel, blk, q0, nq),
        out_shape=(shape, pltpu.VMEM((8, 128), F32)) + (pltpu.VMEM((ABD, HEAD), F32),) * more,
        in_specs=[smem(), vmem, vmem, pl.BlockSpec(memory_space=pltpu.HBM)] + [vmem] * len(heads),
        out_specs=(vmem,) * (2 + more),
        scratch_shapes=[
            pltpu.VMEM((ABD, max(start_of(q0 + nq - 1) + SPAN - start_of(q0 + 2), 128)), F32),
            pltpu.VMEM((ABS, SPAN), BF),
            pltpu.VMEM((ABS, SPAN), BF),
            pltpu.VMEM((5, 512, WIN), BF),
            pltpu.VMEM((5, 512, WIN), BF),
            pltpu.SemaphoreType.DMA((nq // 2,)),
        ]
        + [pltpu.VMEM((ABD, HEAD), F32), pltpu.SemaphoreType.DMA((2,))] * (not q0),
        compiler_params=pltpu.CompilerParams(vmem_limit_bytes=SORT_VMEM),
        cost_estimate=pl.CostEstimate(flops=nq * 5 * 2 * ABS * 512 * 512, bytes_accessed=nq * 1300000, transcendentals=0),
        name="sort_ints",
    )(virt, aux, tail, in_hbm(ints), *heads)


def contract(rows, pieces, parts):
    widths = tuple(p[0].shape[2] for p in parts)
    flat = [p[0] for p in parts]
    vmem = pl.BlockSpec(memory_space=pltpu.VMEM)
    hbm = pl.BlockSpec(memory_space=pl.ANY)
    return pl.pallas_call(
        functools.partial(main_kernel, rows, widths),
        out_shape=jax.ShapeDtypeStruct((8, 40, 128), F32),
        in_specs=[vmem] * (8 + len(flat)) + [hbm] * len(parts),
        out_specs=vmem,
        scratch_shapes=[
            pltpu.VMEM((OP, PAY), BF),
            pltpu.VMEM((OP, PAY), BF),
            pltpu.VMEM((ABD, OP), F32),
            pltpu.VMEM((8, OP), F32),
            pltpu.VMEM((OP, ABP), F32),
        ],
        compiler_params=pltpu.CompilerParams(vmem_limit_bytes=VMEM_LIMIT),
        cost_estimate=pl.CostEstimate(flops=3 * 2 * 1280 * 2560 * 256, bytes_accessed=16000000, transcendentals=0),
        name="contract",
    )(*pieces, *[pltpu.with_memory_space_constraint(x, pltpu.VMEM) for x in flat], *[p[1] for p in parts])


def at(x, y, core):
    return ((x % 4) * 4 + y % 4) * 2 + core


def walk(hop, second):
    pairs = []
    for x in range(4):
        for y in range(4):
            for core in range(2):
                along_x = (core == 0) != second
                to = at(x + hop, y, core) if along_x else at(x, y + hop, core)
                pairs.append((at(x, y, core), to))
    return pairs


SWAP = [(i, i ^ 1) for i in range(32)]


def body(amplitudes, pair_irrep, virt_irrep, resid_in, ladder_ints):
    blk = functools.partial(lax.axis_index, "blk")
    hold = lax.optimization_barrier
    pay, four, aux, tail = compact(blk, virt_irrep, pair_irrep, amplitudes, ladder_ints)

    def sort(q0, nq, aux, head=None):
        return list(sort_part(blk, q0, nq, virt_irrep, aux, tail, head, ladder_ints))

    line = [lax.ppermute(pay, "rows", walk(h, False)) for h in HOPS[1:]]
    parts = [sort(*PARTS[0], aux)]
    line, parts[0][1], aux = hold((line, parts[0][1], aux))
    for i, x in enumerate(line):
        four = lax.dynamic_update_slice(four, x, (OJ * (i + 1), 0))
    near = [lax.ppermute(four, "rows", walk(h, True)) for h in HOPS[1:]]
    far = [lax.ppermute(four, "rows", SWAP)]
    parts.append(sort(*PARTS[1], aux, parts[0][2]))
    near, parts[1][1], aux = hold((near, parts[1][1], aux))
    far += [lax.ppermute(p, "rows", SWAP) for p in near]
    parts.append(sort(*PARTS[2], aux, parts[1][2]))
    terms = contract(functools.partial(lax.axis_index, "rows"), [four] + near + far, parts)
    return finish(lax.all_to_all(terms, "blk", 0, 0), resid_in)


def solution(mesh):
    placed = (P("rows", "blk"), P("rows"), P(), P("blk", "rows"), P("rows", "blk"))
    return jax.shard_map(
        body, mesh=mesh, in_specs=placed, out_specs=P("blk", "rows"), check_vma=False
    )
```

```python
import functools

import jax
import jax.numpy as jnp
from jax import lax
from jax.experimental import pallas as pl
from jax.experimental.pallas import tpu as pltpu
from jax.sharding import PartitionSpec as P

BF = jnp.bfloat16
F32 = jnp.float32
I32 = jnp.int32

NV = 400
NI = 8
PER = 50
CN = 50
WIN = 512
OJ = 8
OP = 256
ABD = 152
ABP = 160
ABS = 2 * ABD
PAY = 2560
GRP = 10
SPAN = 2176
HEAD = 4224
CD = CN * NV
EDGE = CD // 128 * 128
HOPS = (0, 2, 1, 3)
PARTS = ((0, 2), (2, 6), (8, 2))
SECT = 8
VMEM_LIMIT = 24 * 1024 * 1024
COMPACT_VMEM = 56 * 1024 * 1024
SORT_VMEM = 22 * 1024 * 1024


def nt(a, b):
    return lax.dot_general(a, b, (((1,), (1,)), ((), ())), preferred_element_type=F32)


def split(x):
    hi = x.astype(BF)
    return hi, (x - hi.astype(F32)).astype(BF)


def where_in_lanes(lane, pieces):
    out = pieces[-1][1]
    for edge, x in reversed(pieces[:-1]):
        out = jnp.where(lane < edge, x, out)
    return out


def turn(lane, x):
    moved = jnp.where(lane < 62, pltpu.roll(x, 65, 1), pltpu.roll(x, 62, 1))
    return jnp.where(lane < 125, moved, 0.0)


def compact_kernel(blk, virt_s, pair_s, virt_v, amp, edge, pays, four, aux, tail, pay, sems):
    c0 = blk() * CN
    lane = lax.broadcasted_iota(I32, (8, WIN), 1)
    sub = lax.broadcasted_iota(I32, (8, WIN), 0)
    irrep = jnp.concatenate([virt_v[...], jnp.full((1, WIN - NV), -1, I32)], axis=1)
    irrep = jnp.broadcast_to(irrep, (8, WIN))
    member = irrep == sub
    before = lax.broadcasted_iota(I32, (WIN, WIN), 0) < lax.broadcasted_iota(I32, (WIN, WIN), 1)
    count = jnp.dot(
        jnp.where(member, 1.0, 0.0).astype(BF),
        jnp.where(before, 1.0, 0.0).astype(BF),
        preferred_element_type=F32,
    )
    rank = jnp.sum(jnp.where(member, count, 0.0), axis=0, keepdims=True).astype(I32)
    rank = jnp.where(lane < NV, jnp.broadcast_to(rank, (8, WIN)), -1)
    tail[...] = jnp.where(lax.broadcasted_iota(I32, (ABD, 128), 1) < CD - EDGE, edge[...], 0.0)
    pair = jnp.zeros((8, WIN), I32)
    for i in range(OJ):
        pair = jnp.where(sub == i, pair_s[i], pair)
    need = jnp.where(lane < NV, jnp.bitwise_xor(irrep, pair), -1)
    row = lax.broadcasted_iota(I32, (128, WIN), 0)
    rows = {}
    for v in range(8):
        need_v = pltpu.roll(need, 16 * v, 1) if v else need
        rank_v = pltpu.roll(rank, 16 * v, 1) if v else rank
        aux[v, 0:8, :] = rank_v
        aux[v, 8:16, :] = pltpu.roll(irrep, 16 * v, 1) if v else irrep
        pick = jnp.where(jnp.broadcast_to(rank_v[0:1, :], (128, WIN)) == row, 1.0, 0.0).astype(BF)
        cs = list(range(v, CN, 8))
        xs = []
        for c in cs:
            first = (NV * c) // 128 * 128
            width = min(WIN, CD - first)
            x = amp[:, first : first + width]
            if width < WIN:
                x = jnp.concatenate([x, jnp.zeros((8, WIN - width), F32)], axis=1)
            xs.append(jnp.where(need_v == virt_s[c0 + c], x, 0.0))
        if len(xs) % 2:
            xs.append(jnp.zeros((8, WIN), F32))
        hi, lo = split(jnp.concatenate(xs, axis=0))
        r = nt(hi, pick) + nt(lo, pick)
        for i, c in enumerate(cs):
            rows[c] = r[8 * i : 8 * i + 8, :]
    lane = lax.broadcasted_iota(I32, (8, 128), 1)
    odd = jnp.bitwise_and(pair[:, 0:128], 1) == 1
    for q in range(GRP):
        r0, r1, r2, r3, r4 = (rows[5 * q + e] for e in range(5))
        r1 = pltpu.roll(r1, 50, 1)
        r2a = pltpu.roll(r2, 100, 1)
        r2b = pltpu.roll(r2, 103, 1)
        r3 = pltpu.roll(r3, 25, 1)
        r4 = pltpu.roll(r4, 75, 1)
        a = where_in_lanes(lane, [(50, r0), (100, r1), (125, r2a), (128, jnp.zeros_like(r0))])
        b = where_in_lanes(lane, [(25, r2b), (75, r3), (128, r4)])
        a = jnp.where(odd, turn(lane, a), a)
        b = jnp.where(odd, turn(lane, b), b)
        if q == GRP - 1:
            b = jnp.where(lane == 127, pair[:, 0:128].astype(F32), b)
        pay[:, 256 * q : 256 * q + 128] = a
        pay[:, 256 * q + 128 : 256 * q + 256] = b
    copies = [
        pltpu.make_async_copy(pay, pays, sems.at[0]),
        pltpu.make_async_copy(pay, four.at[pl.ds(0, OJ), :], sems.at[1]),
    ]
    for c in copies:
        c.start()
    for c in copies:
        c.wait()


def start_of(q):
    return NV * 5 * q // 128 * 128


def chunks(q0, nq):
    edges = [start_of(q0 + 2)] + [min(start_of(q) + SPAN, EDGE) for q in range(q0 + 3, q0 + nq, 2)]
    return [(a, b - a) for a, b in zip(edges, edges[1:])]


def sort_kernel(blk, q0, nq, virt_s, aux, tail, ints, *refs):
    if q0:
        head, *refs = refs
    else:
        *refs, head, head_sems = refs
    both, done = refs[:2]
    x, ba, bb, ma, mb, sems = refs[-6:]
    c0 = blk() * CN
    spans = chunks(q0, nq)
    base = start_of(q0 + 2)
    copies = [
        pltpu.make_async_copy(
            ints.at[:, pl.ds(first, width)], x.at[:, pl.ds(first - base, width)], sems.at[j]
        )
        for j, (first, width) in enumerate(spans)
    ]
    if q0 + nq < GRP:
        wide = min(HEAD, EDGE - start_of(q0 + nq))
        copies.append(pltpu.make_async_copy(ints.at[:, pl.ds(start_of(q0 + nq), wide)], refs[2].at[:, pl.ds(0, wide)], sems.at[nq // 2 - 1]))
    first = []
    if not q0:
        first = [
            pltpu.make_async_copy(ints.at[:, pl.ds(a, w)], head.at[:, pl.ds(a, w)], head_sems.at[j])
            for j, (a, w) in enumerate(((0, SPAN), (SPAN, HEAD - SPAN)))
        ]
    for c in first + copies:
        c.start()
    if q0 + nq == GRP and nq > 2:
        x[:, EDGE - base : EDGE - base + 128] = tail[...]
    row = lax.broadcasted_iota(I32, (128, WIN), 0)
    lane = lax.broadcasted_iota(I32, (ABS, 128), 1)
    turned = jnp.where(lane < 62, lane + 63, lane - 62).astype(F32).astype(BF)
    lane = lane.astype(F32).astype(BF)

    def load(i, b):
        begin = start_of(q0 + i) - start_of(q0 + i // 2 * 2 if i < 2 else q0 + 2)
        w = (head if i < 2 else x)[:, begin : begin + SPAN]
        if q0 + i == GRP - 1 and i < 2:
            w = jnp.concatenate([w[:, : SPAN - 128], tail[...]], axis=1)
        hi = w.astype(BF).astype(F32)
        b[...] = jnp.concatenate([hi, w - hi], axis=0).astype(BF)

    def build(i, e, m):
        v = (5 * (q0 + i) + e) % 8
        rank = aux[v, 0:8, :]
        irrep = aux[v, 8:16, :]
        inside = rank >= 0
        sector = jnp.bitwise_xor(irrep, virt_s[c0 + 5 * (q0 + i) + e])
        place = rank + 50 * e
        place = jnp.where(place >= 125, place - 125, place)
        place = place + 62 * jnp.bitwise_and(sector, 1)
        place = jnp.where(place >= 125, place - 125, place)
        place = jnp.where(inside, place, -1)
        pick = jnp.where(jnp.broadcast_to(place[0:1, :], (128, WIN)) == row, 1.0, 0.0).astype(BF)
        half = jnp.where(inside, lax.shift_right_logical(sector, 1), -1)
        for u in range(4):
            on = jnp.where(half[0:1, :] == u, 1.0, 0.0).astype(BF)
            m[e, 128 * u : 128 * u + 128, :] = pick * jnp.broadcast_to(on, (128, WIN))

    def sort(i, e, b, m, built=False):
        if not built:
            build(i, e, m)
        at = NV * 5 * (q0 + i) - start_of(q0 + i) + NV * e
        first = at // 128 * 128
        return nt(b[:, first : first + WIN], m[e]).astype(BF)

    def merge(i, u, parts):
        to = 256 * i
        r = [p[:, 128 * u : 128 * u + 128] for p in parts]
        for odd in range(2):
            at = turned if odd else lane
            for t in range(2):
                edges = [(50, r[0]), (100, r[1]), (128, r[2])] if t == 0 else [(25, r[2]), (75, r[3]), (128, r[4])]
                y = where_in_lanes(at, edges)
                both[2 * u + odd, :, to + 128 * t : to + 128 * t + 128] = y

    def pair(k):
        i = 2 * k
        if k:
            copies[k - 1].wait()
        if first and not k:
            for e in range(5):
                build(i, e, ma)
                build(i + 1, e, mb)
            first[0].wait()
            load(i, ba)
            pa = [sort(i, e, ba, ma, True) for e in range(2)]
            first[1].wait()
            load(i + 1, bb)
            pa += [sort(i, e, ba, ma, True) for e in range(2, 5)]
        else:
            load(i, ba)
            load(i + 1, bb)
            pa = [sort(i, e, ba, ma) for e in range(5)]
        pb = []
        for e in range(5):
            pb.append(sort(i + 1, e, bb, mb, bool(first) and not k))
            if e < 4:
                merge(i, e, pa)
        for u in range(4):
            merge(i + 1, u, pb)

    for k in range(nq // 2):
        pair(k)
    for c in copies[nq // 2 - 1 :]:
        c.wait()
    done[...] = jnp.zeros_like(done)


def main_kernel(rows, widths, *refs):
    n = len(widths)
    pieces = refs[:8]
    ls = refs[8 : 8 + n]
    out, ghi, glo, acc, pair, order = refs[8 + 2 * n :]
    for j in range(8):
        x = pieces[j][...]
        hi, lo = split(x)
        ghi[32 * j : 32 * j + 32, :] = hi
        glo[32 * j : 32 * j + 32, :] = lo
    last = jnp.concatenate([p[:, PAY - 128 : PAY] for p in pieces], axis=0)
    pair[...] = jnp.transpose(last)[120:128, :]
    acc[...] = jnp.zeros_like(acc)

    def some(step, carry):
        total = None
        k = 0
        for i, w in enumerate(widths):
            both = ls[i][pl.ds(SECT * step, SECT)]
            x = nt(both.reshape(SECT * ABS, w), ghi[:, k : k + w])
            y = nt(both[:, 0:ABP].reshape(SECT * ABP, w), glo[:, k : k + w])
            total = (x, y) if total is None else (total[0] + x, total[1] + y)
            k += w
        part = acc[...]
        for i in range(SECT):
            x, y = total[0][ABS * i : ABS * i + ABS], total[1][ABP * i : ABP * i + ABD]
            own = jnp.broadcast_to(pair[7:8, :], (ABD, OP)) == (SECT * step + i).astype(F32)
            part = part + jnp.where(own, x[0:ABD] + x[ABD:ABS] + y, 0.0)
        acc[...] = part
        return carry

    lax.fori_loop(0, NI // SECT, some, 0)
    t = jnp.transpose(jnp.concatenate([acc[...], jnp.zeros((ABP - ABD, OP), F32)], axis=0))
    me = rows()
    core, y, x = lax.rem(me, 2), lax.rem(me // 2, 4), me // 8
    for j in range(8):
        kind = core if j < 4 else 1 - core
        for i in range(4):
            d1, d2 = HOPS[i], HOPS[j % 4]
            dx = jnp.where(kind == 0, d1, d2)
            dy = jnp.where(kind == 0, d2, d1)
            shard = (lax.rem(x + 4 - dx, 4) * 4 + lax.rem(y + 4 - dy, 4)) * 2 + kind
            to = pl.multiple_of(shard * OJ, OJ)
            order[pl.ds(to, OJ), :] = t[32 * j + 8 * i : 32 * j + 8 * i + 8, :]
    for b in range(8):
        out[b, 0:32, :] = order[32 * b : 32 * b + 32, 0:128]
        rest = [order[32 * b + 8 * g : 32 * b + 8 * g + 8, 128:ABP] for g in range(4)]
        out[b, 32:40, :] = jnp.concatenate(rest, axis=1)


def finish(got, resid):
    total = jnp.sum(got, axis=0)
    rest = [total[32:40, 32 * g : 32 * g + ABD - 128] for g in range(4)]
    return resid + jnp.concatenate([total[0:32], jnp.concatenate(rest, axis=0)], axis=1)


def smem():
    return pl.BlockSpec(memory_space=pltpu.SMEM)


def in_hbm(x):
    return pltpu.with_memory_space_constraint(x, pltpu.HBM)


def whole(shape):
    return pl.BlockSpec(shape, lambda g: (0,) * len(shape))


def compact(blk, virt, pair, amp, ints):
    return pl.pallas_call(
        functools.partial(compact_kernel, blk),
        out_shape=(
            pltpu.VMEM((OJ, PAY), F32),
            pltpu.VMEM((4 * OJ, PAY), F32),
            pltpu.VMEM((8, 16, WIN), I32),
            pltpu.VMEM((ABD, 128), F32),
        ),
        grid=(1,),
        in_specs=[
            smem(),
            smem(),
            whole((1, NV)),
            whole((OJ, CD)),
            pl.BlockSpec((ABD, 128), lambda g: (0, EDGE // 128)),
        ],
        out_specs=(
            pl.BlockSpec(memory_space=pl.ANY),
            pl.BlockSpec(memory_space=pl.ANY),
            whole((8, 16, WIN)),
            whole((ABD, 128)),
        ),
        scratch_shapes=[pltpu.VMEM((OJ, PAY), F32), pltpu.SemaphoreType.DMA((2,))],
        compiler_params=pltpu.CompilerParams(vmem_limit_bytes=COMPACT_VMEM),
        name="compact",
    )(virt, pair, virt.reshape(1, NV), in_hbm(amp), in_hbm(ints))


def sort_part(blk, q0, nq, virt, aux, tail, head, ints):
    shape = pltpu.VMEM((NI, ABS, 256 * nq), BF)
    vmem = pl.BlockSpec(memory_space=pltpu.VMEM)
    more = q0 + nq < GRP
    heads = [head] if q0 else []
    return pl.pallas_call(
        functools.partial(sort_kernel, blk, q0, nq),
        out_shape=(shape, pltpu.VMEM((8, 128), F32)) + (pltpu.VMEM((ABD, HEAD), F32),) * more,
        in_specs=[smem(), vmem, vmem, pl.BlockSpec(memory_space=pltpu.HBM)] + [vmem] * len(heads),
        out_specs=(vmem,) * (2 + more),
        scratch_shapes=[
            pltpu.VMEM((ABD, max(start_of(q0 + nq - 1) + SPAN - start_of(q0 + 2), 128)), F32),
            pltpu.VMEM((ABS, SPAN), BF),
            pltpu.VMEM((ABS, SPAN), BF),
            pltpu.VMEM((5, 512, WIN), BF),
            pltpu.VMEM((5, 512, WIN), BF),
            pltpu.SemaphoreType.DMA((nq // 2,)),
        ]
        + [pltpu.VMEM((ABD, HEAD), F32), pltpu.SemaphoreType.DMA((2,))] * (not q0),
        compiler_params=pltpu.CompilerParams(vmem_limit_bytes=SORT_VMEM),
        cost_estimate=pl.CostEstimate(flops=nq * 5 * 2 * ABS * 512 * 512, bytes_accessed=nq * 1300000, transcendentals=0),
        name="sort_ints",
    )(virt, aux, tail, in_hbm(ints), *heads)


def contract(rows, pieces, parts):
    widths = tuple(p[0].shape[2] for p in parts)
    flat = [p[0] for p in parts]
    vmem = pl.BlockSpec(memory_space=pltpu.VMEM)
    hbm = pl.BlockSpec(memory_space=pl.ANY)
    return pl.pallas_call(
        functools.partial(main_kernel, rows, widths),
        out_shape=jax.ShapeDtypeStruct((8, 40, 128), F32),
        in_specs=[vmem] * (8 + len(flat)) + [hbm] * len(parts),
        out_specs=vmem,
        scratch_shapes=[
            pltpu.VMEM((OP, PAY), BF),
            pltpu.VMEM((OP, PAY), BF),
            pltpu.VMEM((ABD, OP), F32),
            pltpu.VMEM((8, OP), F32),
            pltpu.VMEM((OP, ABP), F32),
        ],
        compiler_params=pltpu.CompilerParams(vmem_limit_bytes=VMEM_LIMIT),
        cost_estimate=pl.CostEstimate(flops=3 * 2 * 1280 * 2560 * 256, bytes_accessed=16000000, transcendentals=0),
        name="contract",
    )(*pieces, *[pltpu.with_memory_space_constraint(x, pltpu.VMEM) for x in flat], *[p[1] for p in parts])


def at(x, y, core):
    return ((x % 4) * 4 + y % 4) * 2 + core


def walk(hop, second):
    pairs = []
    for x in range(4):
        for y in range(4):
            for core in range(2):
                along_x = (core == 0) != second
                to = at(x + hop, y, core) if along_x else at(x, y + hop, core)
                pairs.append((at(x, y, core), to))
    return pairs


SWAP = [(i, i ^ 1) for i in range(32)]


def body(amplitudes, pair_irrep, virt_irrep, resid_in, ladder_ints):
    blk = functools.partial(lax.axis_index, "blk")
    hold = lax.optimization_barrier
    pay, four, aux, tail = compact(blk, virt_irrep, pair_irrep, amplitudes, ladder_ints)

    def sort(q0, nq, aux, head=None):
        return list(sort_part(blk, q0, nq, virt_irrep, aux, tail, head, ladder_ints))

    line = [lax.ppermute(pay, "rows", walk(h, False)) for h in HOPS[1:]]
    parts = [sort(*PARTS[0], aux)]
    line, parts[0][1], aux = hold((line, parts[0][1], aux))
    for i, x in enumerate(line):
        four = lax.dynamic_update_slice(four, x, (OJ * (i + 1), 0))
    near = [lax.ppermute(four, "rows", walk(h, True)) for h in HOPS[1:]]
    parts.append(sort(*PARTS[1], aux, parts[0][2]))
    near, four, parts[1][1], aux = hold((near, four, parts[1][1], aux))
    far = [lax.ppermute(p, "rows", SWAP) for p in [four] + near]
    parts.append(sort(*PARTS[2], aux, parts[1][2]))
    terms = contract(functools.partial(lax.axis_index, "rows"), [four] + near + far, parts)
    return finish(lax.all_to_all(terms, "blk", 0, 0), resid_in)


def solution(mesh):
    placed = (P("rows", "blk"), P("rows"), P(), P("blk", "rows"), P("rows", "blk"))
    return jax.shard_map(
        body, mesh=mesh, in_specs=placed, out_specs=P("blk", "rows"), check_vma=False
    )
```
